32 devices in a mesh: row: 4 (over x, core), col: 8 (over z, y).
Axes of the slice: x: 2, y: 2, z: 4, core: 2. Of those that a mesh axis runs over, the one named last changes fastest.
Arguments:
- src_coords: int32 [3, 65536], P(None, 'row'), may hold values from 0 to 51
- tgt_coords: int32 [3, 65536], P(None, 'col'), may hold values from 0 to 51
- src_mass: int32 [65536], P('row'), may hold values from 1 to 298
- tgt_mass: int32 [65536], P('col'), may hold values from 1 to 298
- tgt_start: float32 [65536], P('col'), may hold values from -10 to 170
- kept_src: int32 [4, 8, 64], P('row', 'col'), may hold values from 0 to 127, as said below
- kept_tgt: int32 [4, 8, 64], P('row', 'col'), may hold values from 0 to 63, as said below
- kept_count: int32 [4, 8], P('row', 'col'), may hold values from 1 to 64, as said below
Outputs:
- src_potential: float32 [65536], P('row')
- tgt_potential: float32 [65536], P('col')
The draws below stay inside these ranges and needn't reach their ends.
Inputs may be any that keep to these rules, and one draw needn't show every extreme that they name: `kept_src`: every source tile lies in a live pair of some device of its row block. Slots at or past a device's count hold pairs that are not live. `kept_tgt`: every target tile lies in a live pair of some device of its column block. `kept_count`: some device has exactly 64 live slots in every draw.
All inputs are finite; a program needn't handle non-finite values.
Results may differ from the reference program's by a relative error of at most 0.0001.
Values sent between devices are 32-bit elements; how exact they have to be, the bound alone decides.
A program may use at most 64 MiB of HBM per device.

```python
import jax
import jax.numpy as jnp
from jax import lax

S_ROW = 16384
T_COL = 8192
KMAX = 64
ITERS = 3
NS = 65536
NT = 65536
N_ROW = 4
N_COL = 8


def cluster_coords(key, voxel_count):
    centre_key, spread_key = jax.random.split(key)
    centres = jax.random.randint(centre_key, (3, voxel_count // 128, 1), 6, 46)
    spread = jax.random.randint(spread_key, (3, voxel_count // 128, 128), -6, 7)
    coords = (centres + spread).reshape(3, voxel_count).astype(jnp.int32)
    coords = coords.at[:, 0].set(0)
    coords = coords.at[:, voxel_count - 1].set(51)
    return coords.astype(jnp.int32)


def rising_mass(key, voxel_count):
    ceiling = 100 + 200 * jnp.arange(voxel_count, dtype=jnp.int32) // voxel_count
    mass = jax.random.randint(key, (voxel_count,), 1, ceiling).astype(jnp.int32)
    mass = mass.at[0].set(1)
    mass = mass.at[voxel_count - 1].set(298)
    return mass.astype(jnp.int32)


def tile_pattern(key):
    base_key = jax.random.fold_in(key, 77)
    rank_key, extra_key, chosen_key = jax.random.split(base_key, 3)
    src_tiles_count = S_ROW // 128
    tgt_tiles_count = T_COL // 128
    cells = src_tiles_count * tgt_tiles_count
    row_index = jnp.arange(N_ROW, dtype=jnp.int32)[:, None, None]
    col_index = jnp.arange(N_COL, dtype=jnp.int32)[None, :, None]
    cell_index = jnp.arange(cells, dtype=jnp.int32)[None, None, :]
    src_cell = cell_index // tgt_tiles_count
    tgt_cell = cell_index % tgt_tiles_count
    needed = (src_cell % N_COL == col_index) & (tgt_cell == src_cell // N_COL % tgt_tiles_count)
    needed = needed | (tgt_cell % N_ROW == row_index) & (src_cell == tgt_cell // N_ROW % src_tiles_count)
    ranking = jax.random.randint(rank_key, (N_ROW, N_COL, cells), 0, cells)
    priority = jnp.where(needed, 0, 1 + ranking) * cells + cell_index
    ordered = jnp.argsort(priority, axis=-1, stable=True)[:, :, :KMAX].astype(jnp.int32)
    needed_count = jnp.sum(needed.astype(jnp.int32), axis=-1)
    extra = jax.random.randint(extra_key, (N_ROW, N_COL), 0, KMAX + 1)
    extra = extra * extra * extra // (KMAX * KMAX)
    counted = jnp.maximum(jnp.minimum(needed_count + extra, KMAX), 1)
    position = jnp.arange(N_ROW * N_COL, dtype=jnp.int32).reshape(N_ROW, N_COL)
    chosen = jax.random.randint(chosen_key, (), 0, N_ROW * N_COL)
    counted = jnp.where(position == chosen, KMAX, counted).astype(jnp.int32)
    return ((ordered // tgt_tiles_count).astype(jnp.int32), (ordered % tgt_tiles_count).astype(jnp.int32), counted)


def draw_src_coords(key, part):
    return cluster_coords(jax.random.fold_in(key, 11), NS)


def draw_tgt_coords(key, part):
    return cluster_coords(jax.random.fold_in(key, 13), NT)


def draw_src_mass(key, part):
    return rising_mass(jax.random.fold_in(key, 21), NS)


def draw_tgt_mass(key, part):
    return rising_mass(jax.random.fold_in(key, 23), NT)


def draw_tgt_start(key, part):
    first_key = jax.random.fold_in(jax.random.fold_in(key, 41), 0)
    return jnp.clip(3.0 * jax.random.normal(first_key, (NT,), jnp.float32), -9.0, 9.0)


def draw_kept_src(key, part):
    return tile_pattern(key)[0]


def draw_kept_tgt(key, part):
    return tile_pattern(key)[1]


def draw_kept_count(key, part):
    return tile_pattern(key)[2]


def setup_inputs(seed: int = 0) -> dict:
    keys = jax.random.split(jax.random.key(seed), 9)
    src_coords = draw_src_coords(jax.random.fold_in(keys[8], 71), 0)
    tgt_coords = draw_tgt_coords(jax.random.fold_in(keys[8], 71), 0)
    src_mass = draw_src_mass(jax.random.fold_in(keys[8], 71), 0)
    tgt_mass = draw_tgt_mass(jax.random.fold_in(keys[8], 71), 0)
    tgt_start = draw_tgt_start(jax.random.fold_in(keys[8], 71), 0)
    kept_src = draw_kept_src(jax.random.fold_in(keys[8], 71), 0)
    kept_tgt = draw_kept_tgt(jax.random.fold_in(keys[8], 71), 0)
    kept_count = draw_kept_count(jax.random.fold_in(keys[8], 71), 0)
    return dict(src_coords=src_coords, tgt_coords=tgt_coords, src_mass=src_mass, tgt_mass=tgt_mass, tgt_start=tgt_start, kept_src=kept_src, kept_tgt=kept_tgt, kept_count=kept_count)


very_negative = -1.0e30
cost_scale = 0.05


def tile_costs(src_grid, tgt_grid, src_ids, tgt_ids):
    src_tiles = jnp.take(src_grid, src_ids, axis=1).astype(jnp.float32)
    tgt_tiles = jnp.take(tgt_grid, tgt_ids, axis=1).astype(jnp.float32)
    square = None
    for component in range(3):
        difference = src_tiles[component][:, :, None] - tgt_tiles[component][:, None, :]
        square = difference * difference if component == 0 else square + difference * difference
    return cost_scale * square


def slot_partials(scores, live_slots, reduce_dim):
    peak_values = jnp.max(scores, axis=reduce_dim)
    totals = jnp.sum(jnp.exp(scores - jnp.expand_dims(peak_values, reduce_dim)), axis=reduce_dim)
    return jnp.where(live_slots[:, None], peak_values, very_negative), jnp.where(live_slots[:, None], totals, 0.0)


def segment_lse(peak_values, totals, tile_ids, tile_count):
    flat_ids = tile_ids.reshape(-1)
    peak_flat = peak_values.reshape(-1, 128)
    total_flat = totals.reshape(-1, 128)
    tile_peak = jax.ops.segment_max(peak_flat, flat_ids, num_segments=tile_count)
    weighted = total_flat * jnp.exp(peak_flat - tile_peak[flat_ids])
    tile_total = jax.ops.segment_sum(weighted, flat_ids, num_segments=tile_count)
    return tile_peak.reshape(-1) + jnp.log(tile_total.reshape(-1))


def reference(src_coords, tgt_coords, src_mass, tgt_mass, tgt_start, kept_src, kept_tgt, kept_count):
    src_tiles_count = S_ROW // 128
    tgt_tiles_count = T_COL // 128
    row_index = jnp.arange(N_ROW, dtype=jnp.int32)[:, None, None]
    col_index = jnp.arange(N_COL, dtype=jnp.int32)[None, :, None]
    global_src = (row_index * src_tiles_count + kept_src).reshape(N_ROW * N_COL, KMAX).astype(jnp.int32)
    global_tgt = (col_index * tgt_tiles_count + kept_tgt).reshape(N_ROW * N_COL, KMAX).astype(jnp.int32)
    live_all = (jnp.arange(KMAX, dtype=jnp.int32)[None, None, :] < kept_count[:, :, None]).reshape(N_ROW * N_COL, KMAX)
    src_weight = src_mass.astype(jnp.float32)
    tgt_weight = tgt_mass.astype(jnp.float32)
    src_log = jnp.log(src_weight) - jnp.log(jnp.sum(src_weight))
    tgt_log = jnp.log(tgt_weight) - jnp.log(jnp.sum(tgt_weight))
    src_grid = src_coords.reshape(3, NS // 128, 128)
    tgt_grid = tgt_coords.reshape(3, NT // 128, 128)
    tgt_potential = tgt_start
    src_potential = None
    for iteration in range(ITERS):
        tgt_table = tgt_potential.reshape(-1, 128)

        def row_terms(batch):
            ids_src, ids_tgt, live_slots = batch
            cost = tile_costs(src_grid, tgt_grid, ids_src, ids_tgt)
            picked = jnp.take(tgt_table, ids_tgt, axis=0)
            return slot_partials(picked[:, None, :] - cost, live_slots, 2)

        peak_values, totals = lax.map(row_terms, (global_src, global_tgt, live_all))
        src_potential = src_log - segment_lse(peak_values, totals, global_src, NS // 128)
        src_table = src_potential.reshape(-1, 128)

        def col_terms(batch):
            ids_src, ids_tgt, live_slots = batch
            cost = tile_costs(src_grid, tgt_grid, ids_src, ids_tgt)
            picked = jnp.take(src_table, ids_src, axis=0)
            return slot_partials(picked[:, :, None] - cost, live_slots, 1)

        peak_values, totals = lax.map(col_terms, (global_src, global_tgt, live_all))
        tgt_potential = tgt_log - segment_lse(peak_values, totals, global_tgt, NT // 128)
    return src_potential, tgt_potential
```

```python
import functools
import math

import jax
import jax.numpy as jnp
from jax import lax
from jax.experimental import pallas as pl
from jax.experimental.pallas import tpu as pltpu
from jax.sharding import PartitionSpec as P

ITERS = 3
LANES = 128
NEG = -1e30
CENTRE = 26.0
UNROLL = 8
MESH = pl.DeviceIdType.MESH

COST = 0.05
EXP2 = COST * math.log2(math.e)


def slot_order(keys, other, live, tiles):
    slots = keys.shape[0]
    pos = jnp.arange(slots, dtype=jnp.int32)
    rank_key = jnp.where(live, keys * slots + pos, tiles * slots + pos)
    rank = jnp.sum((rank_key[None, :] < rank_key[:, None]).astype(jnp.int32), axis=1)
    hit = rank[None, :] == pos[:, None]
    mine = jnp.sum(jnp.where(hit, keys[None, :], 0), axis=1)
    theirs = jnp.sum(jnp.where(hit, other[None, :], 0), axis=1)
    same = (keys[None, :] == keys[:, None]) & live[None, :] & (pos[None, :] < pos[:, None])
    place = jnp.where(live, jnp.sum(same.astype(jnp.int32), axis=1), -1)
    place = jnp.sum(jnp.where(hit, place[None, :], 0), axis=1)
    tile = jnp.arange(tiles, dtype=jnp.int32)
    upto = jnp.sum(((keys[None, :] <= tile[:, None]) & live[None, :]).astype(jnp.int32), axis=1)
    held = jnp.any((keys[None, :] == tile[:, None]) & live[None, :], axis=1)
    last = jnp.where(held, upto - 1, slots)
    return mine, theirs, last, jnp.broadcast_to(place[:, None], (slots, LANES))


def kernel(
    n_row, n_col,
    idx, place_s, place_t, src_xyz, tgt_xyz, src_mass, tgt_mass, start,
    src_out, tgt_out,
    a_src, b_src, a_tgt, b_tgt, sq_src, sq_tgt, log_src, log_tgt,
    hat_src, hat_tgt, peak, total, runs, send_src, send_tgt, got_src, got_tgt,
    mass_src, mass_tgt, mass_sems, src_sems, tgt_sems,
):
    row, col = lax.axis_index("row"), lax.axis_index("col")
    slots = place_s.shape[0]
    sublane = lax.broadcasted_iota(jnp.int32, (8, LANES), 0)

    barrier = pltpu.get_barrier_semaphore()
    for axis, me, n in (("row", row, n_row), ("col", col, n_col)):
        for off in range(1, n):
            pl.semaphore_signal(
                barrier, inc=1, device_id={axis: lax.rem(me + off, n)}, device_id_type=MESH
            )

    def set_up(xyz, a_ref, b_ref, sq_ref, tp):
        def step(block, carry):
            for u in range(UNROLL):
                t = block * UNROLL + u
                at = pl.ds(pl.multiple_of(t * LANES, LANES), LANES)
                x, y, z = (xyz[d : d + 1, at].astype(jnp.float32) - CENTRE for d in range(3))
                sq_ref[t // tp, pl.ds(t % tp, 1), :] = x * x + y * y + z * z
                rows = jnp.where(
                    sublane == 0, x, jnp.where(sublane == 1, y, jnp.where(sublane == 2, z, 0.0))
                )
                a_ref[t] = rows
                b_ref[t] = jnp.where(sublane < 3, 2.0 * rows, jnp.where(sublane < 6, 1.0, 0.0))
            return carry

        lax.fori_loop(0, a_ref.shape[0] // UNROLL, step, 0)

    tp_src, tp_tgt = hat_src.shape[2], hat_tgt.shape[2]
    set_up(src_xyz, a_src, b_src, sq_src, tp_src)
    set_up(tgt_xyz, a_tgt, b_tgt, sq_tgt, tp_tgt)
    hat_tgt[0] = start[...] * (1.0 / COST) - sq_tgt[...]
    runs[pl.ds(slots, 8), :] = jnp.full((8, LANES), NEG, jnp.float32)
    for mass, held, me in ((src_mass, mass_src, row), (tgt_mass, mass_tgt, col)):
        lane_sum = jnp.sum(jnp.sum(mass[...], axis=0), axis=0, keepdims=True)
        held[me] = jnp.broadcast_to(lane_sum.astype(jnp.float32), (8, LANES))

    pl.semaphore_wait(barrier, n_row + n_col - 2)

    mass_copies = []
    for axis, held, me, n, base in (
        ("row", mass_src, row, n_row, 0), ("col", mass_tgt, col, n_col, n_row - 1),
    ):
        for off in range(1, n):
            copy = pltpu.make_async_remote_copy(
                src_ref=held.at[me], dst_ref=held.at[me],
                send_sem=mass_sems.at[0, base + off - 1], recv_sem=mass_sems.at[1, base + off - 1],
                device_id={axis: lax.rem(me + off, n)}, device_id_type=MESH,
            )
            copy.start()
            mass_copies.append(copy)

    def partials(moving, a_ref, b_ref, in_row, out_row, place, last_row, table, tp_in):
        def step(block, carry):
            for u in range(UNROLL):
                p = block * UNROLL + u
                i_in, i_out = idx[in_row, p], idx[out_row, p]
                hat = jnp.broadcast_to(
                    moving[i_in // tp_in, pl.ds(i_in % tp_in, 1), :], (8, LANES)
                )
                high = hat.astype(jnp.bfloat16).astype(jnp.float32)
                rest = hat - high
                mid = rest.astype(jnp.bfloat16).astype(jnp.float32)
                a = jnp.where(
                    sublane == 3, high,
                    jnp.where(sublane == 4, mid, jnp.where(sublane == 5, rest - mid, a_ref[i_in])),
                ).astype(jnp.bfloat16)
                scores = lax.dot_general(
                    a, b_ref[i_out].astype(jnp.bfloat16), (((0,), (0,)), ((), ())),
                    preferred_element_type=jnp.float32,
                )
                top = jnp.max(scores, axis=0, keepdims=True)
                peak[pl.ds(p, 1), :] = top
                total[pl.ds(p, 1), :] = jnp.sum(
                    jnp.exp2((scores - top) * EXP2), axis=0, keepdims=True
                )
            return carry

        lax.fori_loop(0, slots // UNROLL, step, 0)
        where_in = place[...]
        lse = jnp.where(where_in >= 0, peak[...] * COST + jnp.log(total[...]), NEG)
        reach = 1
        while reach < slots:
            before = pltpu.roll(lse, reach, axis=0)
            both = jnp.maximum(lse, before) + jnp.log(1.0 + jnp.exp(-jnp.abs(lse - before)))
            lse = jnp.where(where_in >= reach, both, lse)
            reach *= 2
        runs[pl.ds(0, slots), :] = lse

        tp = table.shape[1]

        def pick(block, carry):
            for u in range(UNROLL):
                t = block * UNROLL + u
                table[t // tp, pl.ds(t % tp, 1), :] = runs[pl.ds(idx[last_row, t], 1), :]
            return carry

        lax.fori_loop(0, table.shape[0] * tp // UNROLL, pick, 0)

    def exchange(it, axis, me, n, table, got, hats, out_it, log_own, sems):
        def send(stage, src, dst, off):
            copy = pltpu.make_async_remote_copy(
                src_ref=src, dst_ref=dst,
                send_sem=sems.at[it, stage, 0, off - 1], recv_sem=sems.at[it, stage, 1, off - 1],
                device_id={axis: lax.rem(me + off, n)}, device_id_type=MESH,
            )
            copy.start()
            return copy

        first = [
            send(0, table.at[lax.rem(me + off, n)], got.at[it, me], off) for off in range(1, n)
        ]
        for copy in first:
            copy.wait_recv()
        parts = [table[me]] + [got[it, lax.rem(me + off, n)] for off in range(1, n)]
        top = functools.reduce(jnp.maximum, parts)
        summed = functools.reduce(jnp.add, [jnp.exp(part - top) for part in parts])
        hats[out_it, me] = (log_own[...] - (top + jnp.log(summed))) * (1.0 / COST)
        second = [
            send(1, hats.at[out_it, me], hats.at[out_it, me], off) for off in range(1, n)
        ]
        for copy in second:
            copy.wait_recv()
        for copy in first + second:
            copy.wait_send()

    def src_partials(it):
        partials(
            hat_tgt.at[it], a_tgt, b_src, 1, 0, place_s, 4, send_src, tp_tgt
        )

    def mass_logs():
        for copy in mass_copies:
            copy.wait()
        for mass, held, me, out in (
            (src_mass, mass_src, col, log_src), (tgt_mass, mass_tgt, row, log_tgt),
        ):
            whole = jnp.sum(jnp.sum(held[...], axis=0)[0:1, :], axis=1, keepdims=True)
            out[...] = jnp.log(mass[me].astype(jnp.float32)) - jnp.log(whole)

    def iterate(it, carry):
        src_partials(it)
        exchange(it, "col", col, n_col, send_src, got_src, hat_src, it, log_src, src_sems)
        partials(
            hat_src.at[it], a_src, b_tgt, 2, 3, place_t, 5, send_tgt, tp_src
        )
        exchange(it, "row", row, n_row, send_tgt, got_tgt, hat_tgt, it + 1, log_tgt, tgt_sems)
        return carry

    mass_logs()
    lax.fori_loop(0, ITERS, iterate, 0)
    src_out[...] = (hat_src[ITERS - 1] + sq_src[...]) * COST
    tgt_out[...] = (hat_tgt[ITERS] + sq_tgt[...]) * COST


def on_device(
    n_row, n_col,
    src_coords, tgt_coords, src_mass, tgt_mass, tgt_start, kept_src, kept_tgt, kept_count,
):
    src_ids, tgt_ids = kept_src[0, 0], kept_tgt[0, 0]
    slots = src_ids.shape[0]
    src_tiles, tgt_tiles = src_coords.shape[1] // LANES, tgt_coords.shape[1] // LANES
    live = jnp.arange(slots, dtype=jnp.int32) < kept_count[0, 0]
    s_mine, s_theirs, s_last, place_s = slot_order(src_ids, tgt_ids, live, src_tiles)
    t_mine, t_theirs, t_last, place_t = slot_order(tgt_ids, src_ids, live, tgt_tiles)
    width = max(src_tiles, tgt_tiles, slots)
    idx = jnp.stack(
        [
            jnp.pad(ids, (0, width - ids.shape[0]))
            for ids in (s_mine, s_theirs, t_theirs, t_mine, s_last, t_last)
        ]
    )
    src_block = (n_col, src_tiles // n_col, LANES)
    tgt_block = (n_row, tgt_tiles // n_row, LANES)
    f32 = jnp.float32
    vmem = pl.BlockSpec(memory_space=pltpu.VMEM)
    src_out, tgt_out = pl.pallas_call(
        functools.partial(kernel, n_row, n_col),
        out_shape=(
            jax.ShapeDtypeStruct(src_block, f32),
            jax.ShapeDtypeStruct(tgt_block, f32),
        ),
        in_specs=[pl.BlockSpec(memory_space=pltpu.SMEM)] + [vmem] * 7,
        out_specs=(vmem, vmem),
        scratch_shapes=[
            pltpu.VMEM((src_tiles, 8, LANES), f32),
            pltpu.VMEM((src_tiles, 8, LANES), f32),
            pltpu.VMEM((tgt_tiles, 8, LANES), f32),
            pltpu.VMEM((tgt_tiles, 8, LANES), f32),
            pltpu.VMEM(src_block, f32),
            pltpu.VMEM(tgt_block, f32),
            pltpu.VMEM(src_block[1:], f32),
            pltpu.VMEM(tgt_block[1:], f32),
            pltpu.VMEM((ITERS,) + src_block, f32),
            pltpu.VMEM((ITERS + 1,) + tgt_block, f32),
            pltpu.VMEM((slots, LANES), f32),
            pltpu.VMEM((slots, LANES), f32),
            pltpu.VMEM((slots + 8, LANES), f32),
            pltpu.VMEM(src_block, f32),
            pltpu.VMEM(tgt_block, f32),
            pltpu.VMEM((ITERS,) + src_block, f32),
            pltpu.VMEM((ITERS,) + tgt_block, f32),
            pltpu.VMEM((n_row, 8, LANES), f32),
            pltpu.VMEM((n_col, 8, LANES), f32),
            pltpu.SemaphoreType.DMA((2, n_row + n_col - 2)),
            pltpu.SemaphoreType.DMA((ITERS, 2, 2, n_col - 1)),
            pltpu.SemaphoreType.DMA((ITERS, 2, 2, n_row - 1)),
        ],
        compiler_params=pltpu.CompilerParams(
            collective_id=0, has_side_effects=True, vmem_limit_bytes=32 * 1024 * 1024
        ),
        name="sinkhorn",
    )(
        idx, place_s, place_t, src_coords, tgt_coords,
        src_mass.reshape(src_block), tgt_mass.reshape(tgt_block), tgt_start.reshape(tgt_block),
    )
    return src_out.reshape(-1), tgt_out.reshape(-1)


def solution(mesh):
    placed = (
        P(None, "row"), P(None, "col"), P("row"), P("col"), P("col"),
        P("row", "col", None), P("row", "col", None), P("row", "col"),
    )
    return jax.shard_map(
        functools.partial(on_device, mesh.shape["row"], mesh.shape["col"]),
        mesh=mesh, in_specs=placed, out_specs=(P("row"), P("col")), check_vma=False,
    )
```

```python
import functools
import math

import jax
import jax.numpy as jnp
from jax import lax
from jax.experimental import pallas as pl
from jax.experimental.pallas import tpu as pltpu
from jax.sharding import PartitionSpec as P

ITERS = 3
LANES = 128
NEG = -1e30
CENTRE = 26.0
UNROLL = 8
SLOT_UNROLL = 32
MESH = pl.DeviceIdType.MESH

COST = 0.05
EXP2 = COST * math.log2(math.e)


def order_slots(ids, others, live, tiles):
    slots = ids.shape[1]
    lane = lax.broadcasted_iota(jnp.int32, (slots, slots), 1)
    sub = lax.broadcasted_iota(jnp.int32, (slots, slots), 0)

    def column(row):
        spread = jnp.broadcast_to(row, (slots, slots))
        return jnp.sum(jnp.where(lane == sub, spread, 0), axis=1, keepdims=True)

    key = jnp.where(live, ids, tiles) * slots + lane[0:1, :]
    mine = jnp.where(live, ids, tiles)
    key_col, mine_col = column(key), column(mine)
    before = (key < key_col).astype(jnp.int32)
    rank_col = jnp.sum(before, axis=1, keepdims=True)
    after = (key_col < key).astype(jnp.int32)
    rank = jnp.sum(after, axis=0, keepdims=True)
    hit = rank_col == lane
    sorted_ids = jnp.sum(jnp.where(hit, column(ids), 0), axis=0, keepdims=True)
    sorted_others = jnp.sum(jnp.where(hit, column(others), 0), axis=0, keepdims=True)
    earlier = (mine_col == mine) & (sub < lane)
    place = jnp.sum(earlier.astype(jnp.int32), axis=0, keepdims=True)
    place = jnp.where(live, place, -1)
    place = jnp.sum(
        jnp.where(rank == sub, jnp.broadcast_to(place, (slots, slots)), 0), axis=1, keepdims=True
    )
    tile = lax.broadcasted_iota(jnp.int32, (slots, LANES), 1)
    upto = jnp.sum((mine_col <= tile).astype(jnp.int32), axis=0, keepdims=True)
    held = jnp.sum((mine_col == tile).astype(jnp.int32), axis=0, keepdims=True)
    last = jnp.where(held > 0, upto - 1, slots)
    return sorted_ids, sorted_others, last, jnp.broadcast_to(place, (slots, LANES))


def kernel(
    n_row, n_col,
    count, kept_src, kept_tgt, src_xyz_in, tgt_xyz_in, src_mass_in, tgt_mass_in, start_in,
    src_out, tgt_out,
    src_ids, tgt_ids, src_xyz, tgt_xyz, src_mass, tgt_mass, start, load_sems,
    idx_rows, idx, idx_sem, place_s, place_t,
    a_src, b_src, a_tgt, b_tgt, sq_src, sq_tgt, log_src, log_tgt,
    hat_src, hat_tgt, peak, total, runs, send_src, got_src, got_tgt,
    mass_src, mass_tgt, mass_sems, src_sems, tgt_sems,
):
    row, col = lax.axis_index("row"), lax.axis_index("col")
    slots = place_s.shape[0]
    sublane = lax.broadcasted_iota(jnp.int32, (8, LANES), 0)

    loads = [
        pltpu.make_async_copy(src, dst, load_sems.at[k])
        for k, (src, dst) in enumerate((
            (kept_src, src_ids), (kept_tgt, tgt_ids), (src_mass_in, src_mass),
            (tgt_mass_in, tgt_mass), (src_xyz_in, src_xyz), (tgt_xyz_in, tgt_xyz),
            (start_in, start),
        ))
    ]
    for load in loads:
        load.start()

    barrier = pltpu.get_barrier_semaphore()
    for axis, me, n in (("row", row, n_row), ("col", col, n_col)):
        for off in range(1, n):
            pl.semaphore_signal(
                barrier, inc=1, device_id={axis: lax.rem(me + off, n)}, device_id_type=MESH
            )

    for load in loads[:2]:
        load.wait()
    live = lax.broadcasted_iota(jnp.int32, (1, slots), 1) < count[0, 0]
    idx_rows[...] = jnp.zeros_like(idx_rows)
    for k, (ids, others, place, tiles) in enumerate((
        (src_ids, tgt_ids, place_s, a_src.shape[0]), (tgt_ids, src_ids, place_t, a_tgt.shape[0]),
    )):
        mine, theirs, last, place[...] = order_slots(ids[...], others[...], live, tiles)
        idx_rows[3 * k : 3 * k + 1, 0:slots] = mine
        idx_rows[3 * k + 1 : 3 * k + 2, 0:slots] = theirs
        idx_rows[3 * k + 2 : 3 * k + 3, :] = last
    to_scalars = pltpu.make_async_copy(idx_rows, idx, idx_sem)
    to_scalars.start()
    for load in loads[2:4]:
        load.wait()
    for mass, held, me in ((src_mass, mass_src, row), (tgt_mass, mass_tgt, col)):
        lane_sum = jnp.sum(
            mass[...].reshape(-1, LANES), axis=0, keepdims=True
        )
        held[me] = jnp.broadcast_to(lane_sum.astype(jnp.float32), (8, LANES))

    pl.semaphore_wait(barrier, n_row + n_col - 2)

    mass_copies = []
    for axis, held, me, n, base in (
        ("row", mass_src, row, n_row, 0), ("col", mass_tgt, col, n_col, n_row - 1),
    ):
        for off in range(1, n):
            copy = pltpu.make_async_remote_copy(
                src_ref=held.at[me], dst_ref=held.at[me],
                send_sem=mass_sems.at[0, base + off - 1], recv_sem=mass_sems.at[1, base + off - 1],
                device_id={axis: lax.rem(me + off, n)}, device_id_type=MESH,
            )
            copy.start()
            mass_copies.append(copy)

    def set_up(xyz, a_ref, b_ref, sq_ref):
        def step(block, carry):
            for u in range(UNROLL):
                t = block * UNROLL + u
                at = pl.ds(pl.multiple_of(t * LANES, LANES), LANES)
                x, y, z = (xyz[d : d + 1, at].astype(jnp.float32) - CENTRE for d in range(3))
                sq_ref[pl.ds(t, 1), :] = x * x + y * y + z * z
                rows = jnp.where(
                    sublane == 0, x, jnp.where(sublane == 1, y, jnp.where(sublane == 2, z, 0.0))
                )
                a_ref[t] = rows
                b_ref[t] = jnp.where(sublane < 3, 2.0 * rows, jnp.where(sublane < 6, 1.0, 0.0))
            return carry

        lax.fori_loop(0, a_ref.shape[0] // UNROLL, step, 0)

    for load in loads[4:]:
        load.wait()
    set_up(src_xyz, a_src, b_src, sq_src)
    set_up(tgt_xyz, a_tgt, b_tgt, sq_tgt)
    hat_tgt[0] = start[...] * (1.0 / COST) - sq_tgt[...]
    runs[pl.ds(slots, 8), :] = jnp.full((8, LANES), NEG, jnp.float32)
    to_scalars.wait()

    def partials(load_hat, a_ref, b_ref, in_row, out_row, place):
        def step(block, carry):
            for u in range(SLOT_UNROLL):
                p = block * SLOT_UNROLL + u
                i_in, i_out = idx[in_row, p], idx[out_row, p]
                hat = jnp.broadcast_to(load_hat(i_in), (8, LANES))
                high = hat.astype(jnp.bfloat16).astype(jnp.float32)
                rest = hat - high
                mid = rest.astype(jnp.bfloat16).astype(jnp.float32)
                a = jnp.where(
                    sublane == 3, high,
                    jnp.where(sublane == 4, mid, jnp.where(sublane == 5, rest - mid, a_ref[i_in])),
                ).astype(jnp.bfloat16)
                scores = lax.dot_general(
                    a, b_ref[i_out].astype(jnp.bfloat16), (((0,), (0,)), ((), ())),
                    preferred_element_type=jnp.float32,
                )
                top = jnp.max(scores, axis=0, keepdims=True)
                peak[pl.ds(p, 1), :] = top
                total[pl.ds(p, 1), :] = jnp.sum(
                    jnp.exp2((scores - top) * EXP2), axis=0, keepdims=True
                )
            return carry

        lax.fori_loop(0, slots // SLOT_UNROLL, step, 0)
        where_in = place[...]
        lse = jnp.where(where_in >= 0, peak[...] * COST + jnp.log(total[...]), NEG)
        reach = 1
        while reach < slots:
            before = pltpu.roll(lse, reach, axis=0)
            both = jnp.maximum(lse, before) + jnp.log(1.0 + jnp.exp(-jnp.abs(lse - before)))
            lse = jnp.where(where_in >= reach, both, lse)
            reach *= 2
        runs[pl.ds(0, slots), :] = lse

    def send(axis, me, n, off, src, dst, sems):
        copy = pltpu.make_async_remote_copy(
            src_ref=src, dst_ref=dst, send_sem=sems.at[0, off - 1], recv_sem=sems.at[1, off - 1],
            device_id={axis: lax.rem(me + off, n)}, device_id_type=MESH,
        )
        copy.start()
        return copy

    def merged(parts):
        top = functools.reduce(jnp.maximum, parts)
        return top + jnp.log(functools.reduce(jnp.add, [jnp.exp(part - top) for part in parts]))

    def merge_src(it):
        tp = send_src.shape[1]
        first = []
        for off in range(n_col):
            peer = lax.rem(col + 1 + off, n_col)
            for u in range(tp):
                send_src[peer, u : u + 1, :] = runs[pl.ds(idx[2, peer * tp + u], 1), :]
            if off < n_col - 1:
                first.append(send(
                    "col", col, n_col, off + 1,
                    send_src.at[peer], got_src.at[it, col], src_sems.at[it, 0],
                ))
        for copy in first:
            copy.wait_recv()
        parts = [send_src[col]] + [
            got_src[it, lax.rem(col + off, n_col)] for off in range(1, n_col)
        ]
        hat_src[it, col] = (log_src[...] - merged(parts)) * (1.0 / COST)
        mine = hat_src.at[it, col]
        second = [
            send("col", col, n_col, off, mine, mine, src_sems.at[it, 1])
            for off in range(1, n_col)
        ]
        for copy in second:
            copy.wait_recv()
        for copy in first + second:
            copy.wait_send()

    def merge_tgt(it):
        tiles = got_tgt.shape[2]

        def pick(block, carry):
            for u in range(UNROLL * 2):
                t = block * (UNROLL * 2) + u
                got_tgt[it, row, pl.ds(t, 1), :] = runs[pl.ds(idx[5, t], 1), :]
            return carry

        lax.fori_loop(0, tiles // (UNROLL * 2), pick, 0)
        mine = got_tgt.at[it, row]
        copies = [
            send("row", row, n_row, off, mine, mine, tgt_sems.at[it]) for off in range(1, n_row)
        ]
        for copy in copies:
            copy.wait()
        parts = [got_tgt[it, r] for r in range(n_row)]
        hat_tgt[it + 1] = (log_tgt[...] - merged(parts)) * (1.0 / COST)

    def iterate(it, carry):
        partials(lambda t: hat_tgt[it, pl.ds(t, 1), :], a_tgt, b_src, 1, 0, place_s)
        merge_src(it)
        tp = hat_src.shape[2]
        partials(
            lambda t: hat_src[it, t // tp, pl.ds(t % tp, 1), :], a_src, b_tgt, 4, 3, place_t
        )
        merge_tgt(it)
        return carry

    for copy in mass_copies:
        copy.wait()
    src_all = jnp.sum(jnp.sum(mass_src[...], axis=0)[0:1, :], axis=1, keepdims=True)
    tgt_all = jnp.sum(jnp.sum(mass_tgt[...], axis=0)[0:1, :], axis=1, keepdims=True)
    log_src[...] = jnp.log(src_mass[col].astype(jnp.float32)) - jnp.log(src_all)
    log_tgt[...] = jnp.log(tgt_mass[...].astype(jnp.float32)) - jnp.log(tgt_all)
    lax.fori_loop(0, ITERS, iterate, 0)
    src_hat = hat_src[ITERS - 1].reshape(src_out.shape)
    src_out[...] = (src_hat + sq_src[...]) * COST
    tgt_out[...] = (hat_tgt[ITERS] + sq_tgt[...]) * COST


def on_device(
    n_row, n_col,
    src_coords, tgt_coords, src_mass, tgt_mass, tgt_start, kept_src, kept_tgt, kept_count,
):
    slots = kept_src.shape[-1]
    src_tiles, tgt_tiles = src_coords.shape[1] // LANES, tgt_coords.shape[1] // LANES
    src_split = (n_col, src_tiles // n_col, LANES)
    src_block, tgt_block = (src_tiles, LANES), (tgt_tiles, LANES)
    f32, i32 = jnp.float32, jnp.int32
    vmem = pl.BlockSpec(memory_space=pltpu.VMEM)
    src_out, tgt_out = pl.pallas_call(
        functools.partial(kernel, n_row, n_col),
        out_shape=(
            jax.ShapeDtypeStruct(src_block, f32),
            jax.ShapeDtypeStruct(tgt_block, f32),
        ),
        in_specs=[pl.BlockSpec(memory_space=pltpu.SMEM)] + [pl.BlockSpec(memory_space=pl.ANY)] * 7,
        out_specs=(vmem, vmem),
        scratch_shapes=[
            pltpu.VMEM((1, slots), i32),
            pltpu.VMEM((1, slots), i32),
            pltpu.VMEM(src_coords.shape, i32),
            pltpu.VMEM(tgt_coords.shape, i32),
            pltpu.VMEM(src_split, i32),
            pltpu.VMEM(tgt_block, i32),
            pltpu.VMEM(tgt_block, f32),
            pltpu.SemaphoreType.DMA((7,)),
            pltpu.VMEM((8, LANES), i32),
            pltpu.SMEM((8, LANES), i32),
            pltpu.SemaphoreType.DMA,
            pltpu.VMEM((slots, LANES), i32),
            pltpu.VMEM((slots, LANES), i32),
            pltpu.VMEM((src_tiles, 8, LANES), f32),
            pltpu.VMEM((src_tiles, 8, LANES), f32),
            pltpu.VMEM((tgt_tiles, 8, LANES), f32),
            pltpu.VMEM((tgt_tiles, 8, LANES), f32),
            pltpu.VMEM(src_block, f32),
            pltpu.VMEM(tgt_block, f32),
            pltpu.VMEM(src_split[1:], f32),
            pltpu.VMEM(tgt_block, f32),
            pltpu.VMEM((ITERS,) + src_split, f32),
            pltpu.VMEM((ITERS + 1,) + tgt_block, f32),
            pltpu.VMEM((slots, LANES), f32),
            pltpu.VMEM((slots, LANES), f32),
            pltpu.VMEM((slots + 8, LANES), f32),
            pltpu.VMEM(src_split, f32),
            pltpu.VMEM((ITERS,) + src_split, f32),
            pltpu.VMEM((ITERS, n_row) + tgt_block, f32),
            pltpu.VMEM((n_row, 8, LANES), f32),
            pltpu.VMEM((n_col, 8, LANES), f32),
            pltpu.SemaphoreType.DMA((2, n_row + n_col - 2)),
            pltpu.SemaphoreType.DMA((ITERS, 2, 2, n_col - 1)),
            pltpu.SemaphoreType.DMA((ITERS, 2, n_row - 1)),
        ],
        compiler_params=pltpu.CompilerParams(
            collective_id=0, has_side_effects=True, vmem_limit_bytes=48 * 1024 * 1024
        ),
        name="sinkhorn",
    )(
        kept_count, kept_src.reshape(1, slots), kept_tgt.reshape(1, slots),
        src_coords, tgt_coords,
        src_mass.reshape(src_split), tgt_mass.reshape(tgt_block), tgt_start.reshape(tgt_block),
    )
    return src_out.reshape(-1), tgt_out.reshape(-1)


def solution(mesh):
    placed = (
        P(None, "row"), P(None, "col"), P("row"), P("col"), P("col"),
        P("row", "col", None), P("row", "col", None), P("row", "col"),
    )
    return jax.shard_map(
        functools.partial(on_device, mesh.shape["row"], mesh.shape["col"]),
        mesh=mesh, in_specs=placed, out_specs=(P("row"), P("col")), check_vma=False,
    )
```

```python
import functools
import math

import jax
import jax.numpy as jnp
from jax import lax
from jax.experimental import pallas as pl
from jax.experimental.pallas import tpu as pltpu
from jax.sharding import PartitionSpec as P

ITERS = 3
LANES = 128
NEG = -1e30
CENTRE = 26.0
UNROLL = 8
SLOT_UNROLL = 32
MESH = pl.DeviceIdType.MESH

COST = 0.05
EXP2 = COST * math.log2(math.e)


def order_slots(ids, others, live, tiles):
    slots = ids.shape[1]
    lane = lax.broadcasted_iota(jnp.int32, (slots, slots), 1)
    sub = lax.broadcasted_iota(jnp.int32, (slots, slots), 0)

    def column(row):
        spread = jnp.broadcast_to(row, (slots, slots))
        return jnp.sum(jnp.where(lane == sub, spread, 0), axis=1, keepdims=True)

    key = jnp.where(live, ids, tiles) * slots + lane[0:1, :]
    mine = jnp.where(live, ids, tiles)
    key_col, mine_col = column(key), column(mine)
    before = (key < key_col).astype(jnp.int32)
    rank_col = jnp.sum(before, axis=1, keepdims=True)
    after = (key_col < key).astype(jnp.int32)
    rank = jnp.sum(after, axis=0, keepdims=True)
    hit = rank_col == lane
    sorted_ids = jnp.sum(jnp.where(hit, column(ids), 0), axis=0, keepdims=True)
    sorted_others = jnp.sum(jnp.where(hit, column(others), 0), axis=0, keepdims=True)
    earlier = (mine_col == mine) & (sub < lane)
    place = jnp.sum(earlier.astype(jnp.int32), axis=0, keepdims=True)
    place = jnp.where(live, place, -1)
    place = jnp.sum(
        jnp.where(rank == sub, jnp.broadcast_to(place, (slots, slots)), 0), axis=1, keepdims=True
    )
    tile = lax.broadcasted_iota(jnp.int32, (slots, LANES), 1)
    upto = jnp.sum((mine_col <= tile).astype(jnp.int32), axis=0, keepdims=True)
    held = jnp.sum((mine_col == tile).astype(jnp.int32), axis=0, keepdims=True)
    last = jnp.where(held > 0, upto - 1, slots)
    return sorted_ids, sorted_others, last, jnp.broadcast_to(place, (slots, LANES))


def kernel(
    n_row, n_col,
    count, kept_src, kept_tgt, src_xyz_in, tgt_xyz_in, src_mass_in, tgt_mass_in, start_in,
    out,
    live_count, src_ids, tgt_ids, src_xyz, tgt_xyz, src_mass, tgt_mass, start, load_sems,
    idx_rows, idx, idx_sem, place_s, place_t,
    a_src, b_src, a_tgt, b_tgt, sq_src, sq_tgt, log_src, log_tgt,
    hat_src, hat_tgt, peak, total, runs, send_src, got_src, got_tgt,
    mass_src, mass_tgt, mass_sems, src_sems, tgt_sems,
):
    row, col = lax.axis_index("row"), lax.axis_index("col")
    slots = place_s.shape[0]
    sublane = lax.broadcasted_iota(jnp.int32, (8, LANES), 0)

    loads = [
        pltpu.make_async_copy(src, dst, load_sems.at[k])
        for k, (src, dst) in enumerate((
            (kept_src, src_ids), (kept_tgt, tgt_ids), (src_mass_in, src_mass),
            (tgt_mass_in, tgt_mass), (src_xyz_in, src_xyz), (tgt_xyz_in, tgt_xyz),
            (start_in, start), (count, live_count),
        ))
    ]
    for load in loads:
        load.start()

    barrier = pltpu.get_barrier_semaphore()
    for axis, me, n in (("row", row, n_row), ("col", col, n_col)):
        for off in range(1, n):
            pl.semaphore_signal(
                barrier, inc=1, device_id={axis: lax.rem(me + off, n)}, device_id_type=MESH
            )

    for load in loads[:2] + loads[7:]:
        load.wait()
    live = lax.broadcasted_iota(jnp.int32, (1, slots), 1) < live_count[...]
    idx_rows[...] = jnp.zeros_like(idx_rows)
    for k, (ids, others, place, tiles) in enumerate((
        (src_ids, tgt_ids, place_s, a_src.shape[0]), (tgt_ids, src_ids, place_t, a_tgt.shape[0]),
    )):
        mine, theirs, last, place[...] = order_slots(ids[...], others[...], live, tiles)
        idx_rows[3 * k : 3 * k + 1, 0:slots] = mine
        idx_rows[3 * k + 1 : 3 * k + 2, 0:slots] = theirs
        idx_rows[3 * k + 2 : 3 * k + 3, :] = last
    to_scalars = pltpu.make_async_copy(idx_rows, idx, idx_sem)
    to_scalars.start()
    for load in loads[2:4]:
        load.wait()
    for mass, held, me in ((src_mass, mass_src, row), (tgt_mass, mass_tgt, col)):
        lane_sum = jnp.sum(
            mass[...].reshape(-1, LANES), axis=0, keepdims=True
        )
        held[me] = jnp.broadcast_to(lane_sum.astype(jnp.float32), (8, LANES))

    pl.semaphore_wait(barrier, n_row + n_col - 2)

    mass_copies = []
    for axis, held, me, n, base in (
        ("row", mass_src, row, n_row, 0), ("col", mass_tgt, col, n_col, n_row - 1),
    ):
        for off in range(1, n):
            copy = pltpu.make_async_remote_copy(
                src_ref=held.at[me], dst_ref=held.at[me],
                send_sem=mass_sems.at[0, base + off - 1], recv_sem=mass_sems.at[1, base + off - 1],
                device_id={axis: lax.rem(me + off, n)}, device_id_type=MESH,
            )
            copy.start()
            mass_copies.append(copy)

    def set_up(xyz, a_ref, b_ref, sq_ref):
        def step(block, carry):
            for u in range(UNROLL):
                t = block * UNROLL + u
                at = pl.ds(pl.multiple_of(t * LANES, LANES), LANES)
                x, y, z = (xyz[d : d + 1, at].astype(jnp.float32) - CENTRE for d in range(3))
                sq_ref[pl.ds(t, 1), :] = x * x + y * y + z * z
                rows = jnp.where(
                    sublane == 0, x, jnp.where(sublane == 1, y, jnp.where(sublane == 2, z, 0.0))
                )
                a_ref[t] = rows
                b_ref[t] = jnp.where(sublane < 3, 2.0 * rows, jnp.where(sublane < 6, 1.0, 0.0))
            return carry

        lax.fori_loop(0, a_ref.shape[0] // UNROLL, step, 0)

    for load in loads[4:7]:
        load.wait()
    set_up(src_xyz, a_src, b_src, sq_src)
    set_up(tgt_xyz, a_tgt, b_tgt, sq_tgt)
    hat_tgt[0] = start[...] * (1.0 / COST) - sq_tgt[...]
    runs[pl.ds(slots, 8), :] = jnp.full((8, LANES), NEG, jnp.float32)
    to_scalars.wait()

    def partials(load_hat, a_ref, b_ref, in_row, out_row, place):
        def step(block, carry):
            for u in range(0, SLOT_UNROLL, 2):
                lefts, rights = [], []
                for v in range(2):
                    p = block * SLOT_UNROLL + u + v
                    i_in, i_out = idx[in_row, p], idx[out_row, p]
                    hat = jnp.broadcast_to(load_hat(i_in), (8, LANES))
                    high = hat.astype(jnp.bfloat16).astype(jnp.float32)
                    rest = hat - high
                    mid = rest.astype(jnp.bfloat16).astype(jnp.float32)
                    low = rest - mid
                    lefts.append(jnp.where(
                        sublane == 3, high,
                        jnp.where(sublane == 4, mid, jnp.where(sublane == 5, low, a_ref[i_in])),
                    ))
                    zero = jnp.zeros((8, LANES), jnp.float32)
                    pair = [b_ref[i_out], zero] if v == 0 else [zero, b_ref[i_out]]
                    rights.append(jnp.concatenate(pair, axis=1))
                scores = lax.dot_general(
                    jnp.concatenate(lefts, axis=0).astype(jnp.bfloat16),
                    jnp.concatenate(rights, axis=0).astype(jnp.bfloat16),
                    (((0,), (0,)), ((), ())), preferred_element_type=jnp.float32,
                )
                for v in range(2):
                    p = block * SLOT_UNROLL + u + v
                    part = scores[:, v * LANES : (v + 1) * LANES]
                    top = jnp.max(part, axis=0, keepdims=True)
                    peak[pl.ds(p, 1), :] = top
                    total[pl.ds(p, 1), :] = jnp.sum(
                        jnp.exp2((part - top) * EXP2), axis=0, keepdims=True
                    )
            return carry

        lax.fori_loop(0, slots // SLOT_UNROLL, step, 0)
        where_in = place[...]
        top, summed = peak[...], total[...]
        reach = 1
        while reach < slots:
            top_before = pltpu.roll(top, reach, axis=0)
            sum_before = pltpu.roll(summed, reach, axis=0)
            both = jnp.maximum(top, top_before)
            low = jnp.exp2((jnp.minimum(top, top_before) - both) * EXP2)
            here = top >= top_before
            both_sum = jnp.where(here, summed, sum_before) + low * jnp.where(
                here, sum_before, summed
            )
            joined = where_in >= reach
            top, summed = jnp.where(joined, both, top), jnp.where(joined, both_sum, summed)
            reach *= 2
        runs[pl.ds(0, slots), :] = jnp.where(
            where_in >= 0, top * COST + jnp.log(summed), NEG
        )

    def send(axis, me, n, off, src, dst, sems):
        copy = pltpu.make_async_remote_copy(
            src_ref=src, dst_ref=dst, send_sem=sems.at[0, off - 1], recv_sem=sems.at[1, off - 1],
            device_id={axis: lax.rem(me + off, n)}, device_id_type=MESH,
        )
        copy.start()
        return copy

    def merged(parts):
        top = functools.reduce(jnp.maximum, parts)
        return top + jnp.log(functools.reduce(jnp.add, [jnp.exp(part - top) for part in parts]))

    def merge_src(it):
        tp = send_src.shape[1]
        first = []
        for off in range(n_col):
            peer = lax.rem(col + 1 + off, n_col)
            for u in range(tp):
                send_src[peer, u : u + 1, :] = runs[pl.ds(idx[2, peer * tp + u], 1), :]
            if off < n_col - 1:
                first.append(send(
                    "col", col, n_col, off + 1,
                    send_src.at[peer], got_src.at[it, col], src_sems.at[it, 0],
                ))
        for copy in first:
            copy.wait_recv()
        parts = [send_src[col]] + [
            got_src[it, lax.rem(col + off, n_col)] for off in range(1, n_col)
        ]
        hat_src[it, col] = (log_src[...] - merged(parts)) * (1.0 / COST)
        mine = hat_src.at[it, col]
        second = [
            send("col", col, n_col, off, mine, mine, src_sems.at[it, 1])
            for off in range(1, n_col)
        ]
        for copy in second:
            copy.wait_recv()
        for copy in first + second:
            copy.wait_send()

    def merge_tgt(it):
        tiles = got_tgt.shape[2]

        def pick(block, carry):
            for u in range(UNROLL * 2):
                t = block * (UNROLL * 2) + u
                got_tgt[it, row, pl.ds(t, 1), :] = runs[pl.ds(idx[5, t], 1), :]
            return carry

        lax.fori_loop(0, tiles // (UNROLL * 2), pick, 0)
        mine = got_tgt.at[it, row]
        copies = [
            send("row", row, n_row, off, mine, mine, tgt_sems.at[it]) for off in range(1, n_row)
        ]
        for copy in copies:
            copy.wait()
        parts = [got_tgt[it, r] for r in range(n_row)]
        hat_tgt[it + 1] = (log_tgt[...] - merged(parts)) * (1.0 / COST)

    def iterate(it, carry):
        partials(lambda t: hat_tgt[it, pl.ds(t, 1), :], a_tgt, b_src, 1, 0, place_s)
        merge_src(it)
        tp = hat_src.shape[2]
        partials(
            lambda t: hat_src[it, t // tp, pl.ds(t % tp, 1), :], a_src, b_tgt, 4, 3, place_t
        )
        merge_tgt(it)
        return carry

    for copy in mass_copies:
        copy.wait()
    src_all = jnp.sum(jnp.sum(mass_src[...], axis=0)[0:1, :], axis=1, keepdims=True)
    tgt_all = jnp.sum(jnp.sum(mass_tgt[...], axis=0)[0:1, :], axis=1, keepdims=True)
    log_src[...] = jnp.log(src_mass[col].astype(jnp.float32)) - jnp.log(src_all)
    log_tgt[...] = jnp.log(tgt_mass[...].astype(jnp.float32)) - jnp.log(tgt_all)
    lax.fori_loop(0, ITERS, iterate, 0)
    src_tiles = sq_src.shape[0]
    out[0:src_tiles, :] = (hat_src[ITERS - 1].reshape(sq_src.shape) + sq_src[...]) * COST
    out[src_tiles:, :] = (hat_tgt[ITERS] + sq_tgt[...]) * COST


def on_device(
    n_row, n_col,
    src_coords, tgt_coords, src_mass, tgt_mass, tgt_start, kept_src, kept_tgt, kept_count,
):
    slots = kept_src.shape[-1]
    src_tiles, tgt_tiles = src_coords.shape[1] // LANES, tgt_coords.shape[1] // LANES
    src_split = (n_col, src_tiles // n_col, LANES)
    src_block, tgt_block = (src_tiles, LANES), (tgt_tiles, LANES)
    f32, i32 = jnp.float32, jnp.int32
    out = pl.pallas_call(
        functools.partial(kernel, n_row, n_col),
        out_shape=jax.ShapeDtypeStruct((src_tiles + tgt_tiles, LANES), f32),
        in_specs=[pl.BlockSpec(memory_space=pl.ANY)] * 8,
        out_specs=pl.BlockSpec(memory_space=pltpu.VMEM),
        scratch_shapes=[
            pltpu.VMEM((1, 1), i32),
            pltpu.VMEM((1, slots), i32),
            pltpu.VMEM((1, slots), i32),
            pltpu.VMEM(src_coords.shape, i32),
            pltpu.VMEM(tgt_coords.shape, i32),
            pltpu.VMEM(src_split, i32),
            pltpu.VMEM(tgt_block, i32),
            pltpu.VMEM(tgt_block, f32),
            pltpu.SemaphoreType.DMA((8,)),
            pltpu.VMEM((8, LANES), i32),
            pltpu.SMEM((8, LANES), i32),
            pltpu.SemaphoreType.DMA,
            pltpu.VMEM((slots, LANES), i32),
            pltpu.VMEM((slots, LANES), i32),
            pltpu.VMEM((src_tiles, 8, LANES), f32),
            pltpu.VMEM((src_tiles, 8, LANES), f32),
            pltpu.VMEM((tgt_tiles, 8, LANES), f32),
            pltpu.VMEM((tgt_tiles, 8, LANES), f32),
            pltpu.VMEM(src_block, f32),
            pltpu.VMEM(tgt_block, f32),
            pltpu.VMEM(src_split[1:], f32),
            pltpu.VMEM(tgt_block, f32),
            pltpu.VMEM((ITERS,) + src_split, f32),
            pltpu.VMEM((ITERS + 1,) + tgt_block, f32),
            pltpu.VMEM((slots, LANES), f32),
            pltpu.VMEM((slots, LANES), f32),
            pltpu.VMEM((slots + 8, LANES), f32),
            pltpu.VMEM(src_split, f32),
            pltpu.VMEM((ITERS,) + src_split, f32),
            pltpu.VMEM((ITERS, n_row) + tgt_block, f32),
            pltpu.VMEM((n_row, 8, LANES), f32),
            pltpu.VMEM((n_col, 8, LANES), f32),
            pltpu.SemaphoreType.DMA((2, n_row + n_col - 2)),
            pltpu.SemaphoreType.DMA((ITERS, 2, 2, n_col - 1)),
            pltpu.SemaphoreType.DMA((ITERS, 2, n_row - 1)),
        ],
        compiler_params=pltpu.CompilerParams(
            collective_id=0, has_side_effects=True, vmem_limit_bytes=56 * 1024 * 1024
        ),
        name="sinkhorn",
    )(
        kept_count, kept_src.reshape(1, slots), kept_tgt.reshape(1, slots),
        src_coords, tgt_coords,
        src_mass.reshape(src_split), tgt_mass.reshape(tgt_block), tgt_start.reshape(tgt_block),
    )
    return out[:src_tiles].reshape(-1), out[src_tiles:].reshape(-1)


def solution(mesh):
    placed = (
        P(None, "row"), P(None, "col"), P("row"), P("col"), P("col"),
        P("row", "col", None), P("row", "col", None), P("row", "col"),
    )
    return jax.shard_map(
        functools.partial(on_device, mesh.shape["row"], mesh.shape["col"]),
        mesh=mesh, in_specs=placed, out_specs=(P("row"), P("col")), check_vma=False,
    )
```

```python
import functools
import math

import jax
import jax.numpy as jnp
from jax import lax
from jax.experimental import pallas as pl
from jax.experimental.pallas import tpu as pltpu
from jax.sharding import PartitionSpec as P

ITERS = 3
LANES = 128
NEG = -1e30
CENTRE = 26.0
UNROLL = 8
MESH = pl.DeviceIdType.MESH

COST = 0.05
EXP2 = COST * math.log2(math.e)


def order_slots(ids, others, live, tiles):
    slots = ids.shape[1]
    lane = lax.broadcasted_iota(jnp.int32, (slots, slots), 1)
    sub = lax.broadcasted_iota(jnp.int32, (slots, slots), 0)

    def column(row):
        spread = jnp.broadcast_to(row, (slots, slots))
        return jnp.sum(jnp.where(lane == sub, spread, 0), axis=1, keepdims=True)

    key = jnp.where(live, ids, tiles) * slots + lane[0:1, :]
    mine = jnp.where(live, ids, tiles)
    key_col, mine_col = column(key), column(mine)
    before = (key < key_col).astype(jnp.int32)
    rank_col = jnp.sum(before, axis=1, keepdims=True)
    after = (key_col < key).astype(jnp.int32)
    rank = jnp.sum(after, axis=0, keepdims=True)
    hit = rank_col == lane
    sorted_ids = jnp.sum(jnp.where(hit, column(ids), 0), axis=0, keepdims=True)
    sorted_others = jnp.sum(jnp.where(hit, column(others), 0), axis=0, keepdims=True)
    earlier = (mine_col == mine) & (sub < lane)
    place = jnp.sum(earlier.astype(jnp.int32), axis=0, keepdims=True)
    place = jnp.where(live, place, -1)
    place = jnp.sum(
        jnp.where(rank == sub, jnp.broadcast_to(place, (slots, slots)), 0), axis=1, keepdims=True
    )
    tile = lax.broadcasted_iota(jnp.int32, (slots, LANES), 1)
    upto = jnp.sum((mine_col <= tile).astype(jnp.int32), axis=0, keepdims=True)
    held = jnp.sum((mine_col == tile).astype(jnp.int32), axis=0, keepdims=True)
    last = jnp.where(held > 0, upto - 1, slots)
    return sorted_ids, sorted_others, last, jnp.broadcast_to(place, (slots, LANES))


def kernel(
    n_row, n_col,
    count, kept_src, kept_tgt, src_xyz_in, tgt_xyz_in, src_mass_in, tgt_mass_in, start_in,
    src_out, tgt_out,
    live_count, src_ids, tgt_ids, src_xyz, tgt_xyz, src_mass, tgt_mass, start, load_sems,
    idx_rows, idx, idx_sem, place_s, place_t,
    a_src, b_src, a_tgt, b_tgt, sq_src, sq_tgt, log_src, log_tgt,
    hat_src, hat_tgt, peak, total, runs, send_src, got_src, got_tgt,
    mass_src, mass_tgt, mass_sems, src_sems, tgt_sems,
):
    row, col = lax.axis_index("row"), lax.axis_index("col")
    slots = place_s.shape[0]
    sublane = lax.broadcasted_iota(jnp.int32, (8, LANES), 0)

    loads = [
        pltpu.make_async_copy(src, dst, load_sems.at[k])
        for k, (src, dst) in enumerate((
            (kept_src, src_ids), (kept_tgt, tgt_ids), (src_mass_in, src_mass),
            (tgt_mass_in, tgt_mass), (src_xyz_in, src_xyz), (tgt_xyz_in, tgt_xyz),
            (start_in, start), (count, live_count),
        ))
    ]
    for load in loads:
        load.start()

    barrier = pltpu.get_barrier_semaphore()
    for axis, me, n in (("row", row, n_row), ("col", col, n_col)):
        for off in range(1, n):
            pl.semaphore_signal(
                barrier, inc=1, device_id={axis: lax.rem(me + off, n)}, device_id_type=MESH
            )

    for load in loads[:2] + loads[7:]:
        load.wait()
    live = lax.broadcasted_iota(jnp.int32, (1, slots), 1) < live_count[...]
    idx_rows[...] = jnp.zeros_like(idx_rows)
    for k, (ids, others, place, tiles) in enumerate((
        (src_ids, tgt_ids, place_s, a_src.shape[0]), (tgt_ids, src_ids, place_t, a_tgt.shape[0]),
    )):
        mine, theirs, last, place[...] = order_slots(ids[...], others[...], live, tiles)
        idx_rows[3 * k : 3 * k + 1, 0:slots] = mine
        idx_rows[3 * k + 1 : 3 * k + 2, 0:slots] = theirs
        idx_rows[3 * k + 2 : 3 * k + 3, :] = last
    to_scalars = pltpu.make_async_copy(idx_rows, idx, idx_sem)
    to_scalars.start()
    for load in loads[2:4]:
        load.wait()
    for mass, held, me in ((src_mass, mass_src, row), (tgt_mass, mass_tgt, col)):
        lane_sum = jnp.sum(
            mass[...].reshape(-1, LANES), axis=0, keepdims=True
        )
        held[me] = jnp.broadcast_to(lane_sum.astype(jnp.float32), (8, LANES))

    def set_up(xyz, a_ref, b_ref, sq_ref):
        def step(block, carry):
            for u in range(UNROLL):
                t = block * UNROLL + u
                at = pl.ds(pl.multiple_of(t * LANES, LANES), LANES)
                x, y, z = (xyz[d : d + 1, at].astype(jnp.float32) - CENTRE for d in range(3))
                sq_ref[pl.ds(t, 1), :] = x * x + y * y + z * z
                rows = jnp.where(
                    sublane == 0, x, jnp.where(sublane == 1, y, jnp.where(sublane == 2, z, 0.0))
                )
                a_ref[t] = rows
                b_ref[t] = jnp.where(sublane < 3, 2.0 * rows, jnp.where(sublane < 6, 1.0, 0.0))
            return carry

        lax.fori_loop(0, a_ref.shape[0] // UNROLL, step, 0)

    for load in loads[4:7]:
        load.wait()
    set_up(src_xyz, a_src, b_src, sq_src)
    set_up(tgt_xyz, a_tgt, b_tgt, sq_tgt)
    hat_tgt[0] = start[...] * (1.0 / COST) - sq_tgt[...]
    runs[pl.ds(slots, 8), :] = jnp.full((8, LANES), NEG, jnp.float32)

    pl.semaphore_wait(barrier, n_row + n_col - 2)

    mass_copies = []
    for axis, held, me, n, base in (
        ("row", mass_src, row, n_row, 0), ("col", mass_tgt, col, n_col, n_row - 1),
    ):
        for off in range(1, n):
            copy = pltpu.make_async_remote_copy(
                src_ref=held.at[me], dst_ref=held.at[me],
                send_sem=mass_sems.at[0, base + off - 1], recv_sem=mass_sems.at[1, base + off - 1],
                device_id={axis: lax.rem(me + off, n)}, device_id_type=MESH,
            )
            copy.start()
            mass_copies.append(copy)
    to_scalars.wait()

    def partials(load_hat, a_ref, b_ref, in_row, out_row, place):
        for u in range(0, slots, 2):
            lefts, rights = [], []
            for v in range(2):
                p = u + v
                i_in, i_out = idx[in_row, p], idx[out_row, p]
                hat = jnp.broadcast_to(load_hat(i_in), (8, LANES))
                high = hat.astype(jnp.bfloat16).astype(jnp.float32)
                rest = hat - high
                mid = rest.astype(jnp.bfloat16).astype(jnp.float32)
                low = rest - mid
                lefts.append(jnp.where(
                    sublane == 3, high,
                    jnp.where(sublane == 4, mid, jnp.where(sublane == 5, low, a_ref[i_in])),
                ))
                zero = jnp.zeros((8, LANES), jnp.float32)
                pair = [b_ref[i_out], zero] if v == 0 else [zero, b_ref[i_out]]
                rights.append(jnp.concatenate(pair, axis=1))
            scores = lax.dot_general(
                jnp.concatenate(lefts, axis=0).astype(jnp.bfloat16),
                jnp.concatenate(rights, axis=0).astype(jnp.bfloat16),
                (((0,), (0,)), ((), ())), preferred_element_type=jnp.float32,
            )
            for v in range(2):
                p = u + v
                part = scores[:, v * LANES : (v + 1) * LANES]
                top = jnp.max(part, axis=0, keepdims=True)
                peak[pl.ds(p, 1), :] = top
                total[pl.ds(p, 1), :] = jnp.sum(
                    jnp.exp2((part - top) * EXP2), axis=0, keepdims=True
                )
        where_in = place[...]
        top, summed = peak[...], total[...]
        reach = 1
        while reach < slots:
            top_before = pltpu.roll(top, reach, axis=0)
            sum_before = pltpu.roll(summed, reach, axis=0)
            both = jnp.maximum(top, top_before)
            low = jnp.exp2((jnp.minimum(top, top_before) - both) * EXP2)
            here = top >= top_before
            both_sum = jnp.where(here, summed, sum_before) + low * jnp.where(
                here, sum_before, summed
            )
            joined = where_in >= reach
            top, summed = jnp.where(joined, both, top), jnp.where(joined, both_sum, summed)
            reach *= 2
        runs[pl.ds(0, slots), :] = jnp.where(
            where_in >= 0, top * COST + jnp.log(summed), NEG
        )

    def send(axis, me, n, off, src, dst, sems):
        copy = pltpu.make_async_remote_copy(
            src_ref=src, dst_ref=dst, send_sem=sems.at[0, off - 1], recv_sem=sems.at[1, off - 1],
            device_id={axis: lax.rem(me + off, n)}, device_id_type=MESH,
        )
        copy.start()
        return copy

    def merged(parts):
        top = functools.reduce(jnp.maximum, parts)
        return top + jnp.log(functools.reduce(jnp.add, [jnp.exp(part - top) for part in parts]))

    def mass_logs():
        for copy in mass_copies:
            copy.wait()
        src_all = jnp.sum(jnp.sum(mass_src[...], axis=0)[0:1, :], axis=1, keepdims=True)
        tgt_all = jnp.sum(jnp.sum(mass_tgt[...], axis=0)[0:1, :], axis=1, keepdims=True)
        log_src[...] = jnp.log(src_mass[col].astype(jnp.float32)) - jnp.log(src_all)
        log_tgt[...] = jnp.log(tgt_mass[...].astype(jnp.float32)) - jnp.log(tgt_all)

    def merge_src(it):
        tp = send_src.shape[1]
        first = []
        for off in range(n_col):
            peer = lax.rem(col + 1 + off, n_col)
            for u in range(tp):
                send_src[peer, u : u + 1, :] = runs[pl.ds(idx[2, peer * tp + u], 1), :]
            if off < n_col - 1:
                first.append(send(
                    "col", col, n_col, off + 1,
                    send_src.at[peer], got_src.at[it, col], src_sems.at[it, 0],
                ))
        pl.when(it == 0)(mass_logs)
        for copy in first:
            copy.wait_recv()
        parts = [send_src[col]] + [
            got_src[it, lax.rem(col + off, n_col)] for off in range(1, n_col)
        ]
        hat_src[it, col] = (log_src[...] - merged(parts)) * (1.0 / COST)
        mine = hat_src.at[it, col]
        second = [
            send("col", col, n_col, off, mine, mine, src_sems.at[it, 1])
            for off in range(1, n_col)
        ]
        for copy in second:
            copy.wait_recv()
        for copy in first + second:
            copy.wait_send()

    def merge_tgt(it):
        tiles = got_tgt.shape[2]

        def pick(block, carry):
            for u in range(UNROLL * 2):
                t = block * (UNROLL * 2) + u
                got_tgt[it, row, pl.ds(t, 1), :] = runs[pl.ds(idx[5, t], 1), :]
            return carry

        lax.fori_loop(0, tiles // (UNROLL * 2), pick, 0)
        mine = got_tgt.at[it, row]
        copies = [
            send("row", row, n_row, off, mine, mine, tgt_sems.at[it]) for off in range(1, n_row)
        ]
        @pl.when(it == ITERS - 1)
        def _():
            src_hat = hat_src[ITERS - 1].reshape(sq_src.shape)
            src_out[...] = (src_hat + sq_src[...]) * COST

        for copy in copies:
            copy.wait()
        parts = [got_tgt[it, r] for r in range(n_row)]
        hat_tgt[it + 1] = (log_tgt[...] - merged(parts)) * (1.0 / COST)

    def iterate(it, carry):
        partials(lambda t: hat_tgt[it, pl.ds(t, 1), :], a_tgt, b_src, 1, 0, place_s)
        merge_src(it)
        tp = hat_src.shape[2]
        partials(
            lambda t: hat_src[it, t // tp, pl.ds(t % tp, 1), :], a_src, b_tgt, 4, 3, place_t
        )
        merge_tgt(it)
        return carry

    lax.fori_loop(0, ITERS, iterate, 0)
    tgt_out[...] = (hat_tgt[ITERS] + sq_tgt[...]) * COST


def on_device(
    n_row, n_col,
    src_coords, tgt_coords, src_mass, tgt_mass, tgt_start, kept_src, kept_tgt, kept_count,
):
    slots = kept_src.shape[-1]
    src_tiles, tgt_tiles = src_coords.shape[1] // LANES, tgt_coords.shape[1] // LANES
    src_split = (n_col, src_tiles // n_col, LANES)
    src_block, tgt_block = (src_tiles, LANES), (tgt_tiles, LANES)
    f32, i32 = jnp.float32, jnp.int32
    src_out, tgt_out = pl.pallas_call(
        functools.partial(kernel, n_row, n_col),
        out_shape=(
            jax.ShapeDtypeStruct(src_block, f32),
            jax.ShapeDtypeStruct(tgt_block, f32),
        ),
        in_specs=[pl.BlockSpec(memory_space=pl.ANY)] * 8,
        out_specs=(pl.BlockSpec(memory_space=pltpu.VMEM),) * 2,
        scratch_shapes=[
            pltpu.VMEM((1, 1), i32),
            pltpu.VMEM((1, slots), i32),
            pltpu.VMEM((1, slots), i32),
            pltpu.VMEM(src_coords.shape, i32),
            pltpu.VMEM(tgt_coords.shape, i32),
            pltpu.VMEM(src_split, i32),
            pltpu.VMEM(tgt_block, i32),
            pltpu.VMEM(tgt_block, f32),
            pltpu.SemaphoreType.DMA((8,)),
            pltpu.VMEM((8, LANES), i32),
            pltpu.SMEM((8, LANES), i32),
            pltpu.SemaphoreType.DMA,
            pltpu.VMEM((slots, LANES), i32),
            pltpu.VMEM((slots, LANES), i32),
            pltpu.VMEM((src_tiles, 8, LANES), f32),
            pltpu.VMEM((src_tiles, 8, LANES), f32),
            pltpu.VMEM((tgt_tiles, 8, LANES), f32),
            pltpu.VMEM((tgt_tiles, 8, LANES), f32),
            pltpu.VMEM(src_block, f32),
            pltpu.VMEM(tgt_block, f32),
            pltpu.VMEM(src_split[1:], f32),
            pltpu.VMEM(tgt_block, f32),
            pltpu.VMEM((ITERS,) + src_split, f32),
            pltpu.VMEM((ITERS + 1,) + tgt_block, f32),
            pltpu.VMEM((slots, LANES), f32),
            pltpu.VMEM((slots, LANES), f32),
            pltpu.VMEM((slots + 8, LANES), f32),
            pltpu.VMEM(src_split, f32),
            pltpu.VMEM((ITERS,) + src_split, f32),
            pltpu.VMEM((ITERS, n_row) + tgt_block, f32),
            pltpu.VMEM((n_row, 8, LANES), f32),
            pltpu.VMEM((n_col, 8, LANES), f32),
            pltpu.SemaphoreType.DMA((2, n_row + n_col - 2)),
            pltpu.SemaphoreType.DMA((ITERS, 2, 2, n_col - 1)),
            pltpu.SemaphoreType.DMA((ITERS, 2, n_row - 1)),
        ],
        compiler_params=pltpu.CompilerParams(
            collective_id=0, has_side_effects=True, vmem_limit_bytes=56 * 1024 * 1024
        ),
        name="sinkhorn",
    )(
        kept_count, kept_src.reshape(1, slots), kept_tgt.reshape(1, slots),
        src_coords, tgt_coords,
        src_mass.reshape(src_split), tgt_mass.reshape(tgt_block), tgt_start.reshape(tgt_block),
    )
    return src_out.reshape(-1), tgt_out.reshape(-1)


def solution(mesh):
    placed = (
        P(None, "row"), P(None, "col"), P("row"), P("col"), P("col"),
        P("row", "col", None), P("row", "col", None), P("row", "col"),
    )
    return jax.shard_map(
        functools.partial(on_device, mesh.shape["row"], mesh.shape["col"]),
        mesh=mesh, in_specs=placed, out_specs=(P("row"), P("col")), check_vma=False,
    )
```

```python
import functools
import math

import jax
import jax.numpy as jnp
from jax import lax
from jax.experimental import pallas as pl
from jax.experimental.pallas import tpu as pltpu
from jax.sharding import PartitionSpec as P

ITERS = 3
LANES = 128
NEG = -1e30
CENTRE = 26.0
UNROLL = 8
GROUP = 16
MESH = pl.DeviceIdType.MESH

COST = 0.05
EXP2 = COST * math.log2(math.e)


def order_slots(ids, others, live, tiles):
    slots = ids.shape[1]
    lane = lax.broadcasted_iota(jnp.int32, (slots, slots), 1)
    sub = lax.broadcasted_iota(jnp.int32, (slots, slots), 0)

    def column(row):
        spread = jnp.broadcast_to(row, (slots, slots))
        return jnp.sum(jnp.where(lane == sub, spread, 0), axis=1, keepdims=True)

    key = jnp.where(live, ids, tiles) * slots + lane[0:1, :]
    mine = jnp.where(live, ids, tiles)
    key_col, mine_col = column(key), column(mine)
    before = (key < key_col).astype(jnp.int32)
    rank_col = jnp.sum(before, axis=1, keepdims=True)
    after = (key_col < key).astype(jnp.int32)
    rank = jnp.sum(after, axis=0, keepdims=True)
    hit = rank_col == lane
    sorted_ids = jnp.sum(jnp.where(hit, column(ids), 0), axis=0, keepdims=True)
    sorted_others = jnp.sum(jnp.where(hit, column(others), 0), axis=0, keepdims=True)
    earlier = (mine_col == mine) & (sub < lane)
    place = jnp.sum(earlier.astype(jnp.int32), axis=0, keepdims=True)
    place = jnp.where(live, place, -1)
    place = jnp.sum(
        jnp.where(rank == sub, jnp.broadcast_to(place, (slots, slots)), 0), axis=1, keepdims=True
    )
    tile = lax.broadcasted_iota(jnp.int32, (slots, LANES), 1)
    upto = jnp.sum((mine_col <= tile).astype(jnp.int32), axis=0, keepdims=True)
    held = jnp.sum((mine_col == tile).astype(jnp.int32), axis=0, keepdims=True)
    last = jnp.where(held > 0, upto - 1, slots)
    return sorted_ids, sorted_others, last, jnp.broadcast_to(place, (slots, LANES))


def kernel(
    n_row, n_col,
    count, kept_src, kept_tgt, src_xyz_in, tgt_xyz_in, src_mass_in, tgt_mass_in, start_in,
    src_out, tgt_out,
    live_count, src_ids, tgt_ids, src_xyz, tgt_xyz, src_mass, tgt_mass, start, load_sems,
    idx_rows, idx, idx_sem, place_s, place_t,
    a_src, b_src, a_tgt, b_tgt, sq_src, sq_tgt, log_src, log_tgt,
    hat_src, hat_tgt, peak, total, runs, send_src, got_src, got_tgt,
    mass_src, mass_tgt, mass_sems, src_sems, tgt_sems,
):
    row, col = lax.axis_index("row"), lax.axis_index("col")
    slots = place_s.shape[0]
    sublane = lax.broadcasted_iota(jnp.int32, (8, LANES), 0)

    loads = [
        pltpu.make_async_copy(src, dst, load_sems.at[k])
        for k, (src, dst) in enumerate((
            (kept_src, src_ids), (kept_tgt, tgt_ids), (src_mass_in, src_mass),
            (tgt_mass_in, tgt_mass), (src_xyz_in, src_xyz), (tgt_xyz_in, tgt_xyz),
            (start_in, start), (count, live_count),
        ))
    ]
    for load in loads:
        load.start()

    barrier = pltpu.get_barrier_semaphore()
    for axis, me, n in (("row", row, n_row), ("col", col, n_col)):
        for off in range(1, n):
            pl.semaphore_signal(
                barrier, inc=1, device_id={axis: lax.rem(me + off, n)}, device_id_type=MESH
            )

    for load in loads[:2] + loads[7:]:
        load.wait()
    live = lax.broadcasted_iota(jnp.int32, (1, slots), 1) < live_count[...]
    idx_rows[...] = jnp.zeros_like(idx_rows)
    for k, (ids, others, place, tiles) in enumerate((
        (src_ids, tgt_ids, place_s, a_src.shape[0]), (tgt_ids, src_ids, place_t, a_tgt.shape[0]),
    )):
        mine, theirs, last, place[...] = order_slots(ids[...], others[...], live, tiles)
        idx_rows[3 * k : 3 * k + 1, 0:slots] = mine
        idx_rows[3 * k + 1 : 3 * k + 2, 0:slots] = theirs
        idx_rows[3 * k + 2 : 3 * k + 3, :] = last
    to_scalars = pltpu.make_async_copy(idx_rows, idx, idx_sem)
    to_scalars.start()
    for load in loads[2:4]:
        load.wait()
    for mass, held, me in ((src_mass, mass_src, row), (tgt_mass, mass_tgt, col)):
        lane_sum = jnp.sum(
            mass[...].reshape(-1, LANES), axis=0, keepdims=True
        )
        held[me] = jnp.broadcast_to(lane_sum.astype(jnp.float32), (8, LANES))

    def set_up(xyz, a_ref, b_ref, sq_ref):
        def step(block, carry):
            for u in range(UNROLL):
                t = block * UNROLL + u
                at = pl.ds(pl.multiple_of(t * LANES, LANES), LANES)
                x, y, z = (xyz[d : d + 1, at].astype(jnp.float32) - CENTRE for d in range(3))
                sq_ref[pl.ds(t, 1), :] = x * x + y * y + z * z
                rows = jnp.where(
                    sublane == 0, x, jnp.where(sublane == 1, y, jnp.where(sublane == 2, z, 0.0))
                )
                a_ref[t] = rows
                b_ref[t] = jnp.where(sublane < 3, 2.0 * rows, jnp.where(sublane < 6, 1.0, 0.0))
            return carry

        lax.fori_loop(0, a_ref.shape[0] // UNROLL, step, 0)

    for load in loads[4:7]:
        load.wait()
    set_up(src_xyz, a_src, b_src, sq_src)
    set_up(tgt_xyz, a_tgt, b_tgt, sq_tgt)
    hat_tgt[0] = start[...] * (1.0 / COST) - sq_tgt[...]
    runs[pl.ds(slots, 8), :] = jnp.full((8, LANES), NEG, jnp.float32)

    pl.semaphore_wait(barrier, n_row + n_col - 2)

    mass_copies = []
    for axis, held, me, n, base in (
        ("row", mass_src, row, n_row, 0), ("col", mass_tgt, col, n_col, n_row - 1),
    ):
        for off in range(1, n):
            copy = pltpu.make_async_remote_copy(
                src_ref=held.at[me], dst_ref=held.at[me],
                send_sem=mass_sems.at[0, base + off - 1], recv_sem=mass_sems.at[1, base + off - 1],
                device_id={axis: lax.rem(me + off, n)}, device_id_type=MESH,
            )
            copy.start()
            mass_copies.append(copy)
    to_scalars.wait()

    def partials(load_hat, a_ref, b_ref, in_row, out_row, place):
        for first in range(0, slots, GROUP):
            lefts, rights = [], []
            for p in range(first, first + GROUP):
                i_in, i_out = idx[in_row, p], idx[out_row, p]
                hat = jnp.broadcast_to(load_hat(i_in), (8, LANES))
                high = hat.astype(jnp.bfloat16).astype(jnp.float32)
                rest = hat - high
                mid = rest.astype(jnp.bfloat16).astype(jnp.float32)
                low = rest - mid
                lefts.append(jnp.where(
                    sublane == 3, high,
                    jnp.where(sublane == 4, mid, jnp.where(sublane == 5, low, a_ref[i_in])),
                ))
                rights.append(b_ref[i_out])
            left = jnp.concatenate(lefts, axis=0).T.astype(jnp.bfloat16)
            for u in range(0, GROUP, 2):
                zero = jnp.zeros((8, LANES), jnp.float32)
                pair = jnp.concatenate([
                    jnp.concatenate([rights[u], zero], axis=1),
                    jnp.concatenate([zero, rights[u + 1]], axis=1),
                ], axis=0).astype(jnp.bfloat16)
                blocks = [pair]
                if u > 0:
                    blocks.insert(0, jnp.zeros((8 * u, 2 * LANES), jnp.bfloat16))
                if u < GROUP - 2:
                    blocks.append(jnp.zeros((8 * (GROUP - 2 - u), 2 * LANES), jnp.bfloat16))
                scores = jnp.dot(
                    left, jnp.concatenate(blocks, axis=0), preferred_element_type=jnp.float32
                )
                for v in range(2):
                    p = first + u + v
                    part = scores[:, v * LANES : (v + 1) * LANES]
                    top = jnp.max(part, axis=0, keepdims=True)
                    peak[pl.ds(p, 1), :] = top
                    total[pl.ds(p, 1), :] = jnp.sum(
                        jnp.exp2((part - top) * EXP2), axis=0, keepdims=True
                    )
        where_in = place[...]
        top, summed = peak[...], total[...]
        reach = 1
        while reach < slots:
            top_before = pltpu.roll(top, reach, axis=0)
            sum_before = pltpu.roll(summed, reach, axis=0)
            both = jnp.maximum(top, top_before)
            low = jnp.exp2((jnp.minimum(top, top_before) - both) * EXP2)
            here = top >= top_before
            both_sum = jnp.where(here, summed, sum_before) + low * jnp.where(
                here, sum_before, summed
            )
            joined = where_in >= reach
            top, summed = jnp.where(joined, both, top), jnp.where(joined, both_sum, summed)
            reach *= 2
        runs[pl.ds(0, slots), :] = jnp.where(
            where_in >= 0, top * COST + jnp.log(summed), NEG
        )

    def send(axis, me, n, off, src, dst, sems):
        copy = pltpu.make_async_remote_copy(
            src_ref=src, dst_ref=dst, send_sem=sems.at[0, off - 1], recv_sem=sems.at[1, off - 1],
            device_id={axis: lax.rem(me + off, n)}, device_id_type=MESH,
        )
        copy.start()
        return copy

    def merged(parts):
        top = functools.reduce(jnp.maximum, parts)
        return top + jnp.log(functools.reduce(jnp.add, [jnp.exp(part - top) for part in parts]))

    def mass_logs():
        for copy in mass_copies:
            copy.wait()
        src_all = jnp.sum(jnp.sum(mass_src[...], axis=0)[0:1, :], axis=1, keepdims=True)
        tgt_all = jnp.sum(jnp.sum(mass_tgt[...], axis=0)[0:1, :], axis=1, keepdims=True)
        log_src[...] = jnp.log(src_mass[col].astype(jnp.float32)) - jnp.log(src_all)
        log_tgt[...] = jnp.log(tgt_mass[...].astype(jnp.float32)) - jnp.log(tgt_all)

    def merge_src(it):
        tp = send_src.shape[1]
        first = []
        for off in range(n_col):
            peer = lax.rem(col + 1 + off, n_col)
            for u in range(tp):
                send_src[peer, u : u + 1, :] = runs[pl.ds(idx[2, peer * tp + u], 1), :]
            if off < n_col - 1:
                first.append(send(
                    "col", col, n_col, off + 1,
                    send_src.at[peer], got_src.at[it, col], src_sems.at[it, 0],
                ))
        pl.when(it == 0)(mass_logs)
        for copy in first:
            copy.wait_recv()
        parts = [send_src[col]] + [
            got_src[it, lax.rem(col + off, n_col)] for off in range(1, n_col)
        ]
        hat_src[it, col] = (log_src[...] - merged(parts)) * (1.0 / COST)
        mine = hat_src.at[it, col]
        second = [
            send("col", col, n_col, off, mine, mine, src_sems.at[it, 1])
            for off in range(1, n_col)
        ]
        for copy in second:
            copy.wait_recv()
        for copy in first + second:
            copy.wait_send()

    def merge_tgt(it):
        tiles = got_tgt.shape[2]

        def pick(block, carry):
            for u in range(UNROLL * 2):
                t = block * (UNROLL * 2) + u
                got_tgt[it, row, pl.ds(t, 1), :] = runs[pl.ds(idx[5, t], 1), :]
            return carry

        lax.fori_loop(0, tiles // (UNROLL * 2), pick, 0)
        mine = got_tgt.at[it, row]
        copies = [
            send("row", row, n_row, off, mine, mine, tgt_sems.at[it]) for off in range(1, n_row)
        ]
        @pl.when(it == ITERS - 1)
        def _():
            src_hat = hat_src[ITERS - 1].reshape(sq_src.shape)
            src_out[...] = (src_hat + sq_src[...]) * COST

        for copy in copies:
            copy.wait()
        parts = [got_tgt[it, r] for r in range(n_row)]
        hat_tgt[it + 1] = (log_tgt[...] - merged(parts)) * (1.0 / COST)

    def iterate(it, carry):
        partials(lambda t: hat_tgt[it, pl.ds(t, 1), :], a_tgt, b_src, 1, 0, place_s)
        merge_src(it)
        tp = hat_src.shape[2]
        partials(
            lambda t: hat_src[it, t // tp, pl.ds(t % tp, 1), :], a_src, b_tgt, 4, 3, place_t
        )
        merge_tgt(it)
        return carry

    lax.fori_loop(0, ITERS, iterate, 0)
    tgt_out[...] = (hat_tgt[ITERS] + sq_tgt[...]) * COST


def on_device(
    n_row, n_col,
    src_coords, tgt_coords, src_mass, tgt_mass, tgt_start, kept_src, kept_tgt, kept_count,
):
    slots = kept_src.shape[-1]
    src_tiles, tgt_tiles = src_coords.shape[1] // LANES, tgt_coords.shape[1] // LANES
    src_split = (n_col, src_tiles // n_col, LANES)
    src_block, tgt_block = (src_tiles, LANES), (tgt_tiles, LANES)
    f32, i32 = jnp.float32, jnp.int32
    src_out, tgt_out = pl.pallas_call(
        functools.partial(kernel, n_row, n_col),
        out_shape=(
            jax.ShapeDtypeStruct(src_block, f32),
            jax.ShapeDtypeStruct(tgt_block, f32),
        ),
        in_specs=[pl.BlockSpec(memory_space=pl.ANY)] * 8,
        out_specs=(pl.BlockSpec(memory_space=pltpu.VMEM),) * 2,
        scratch_shapes=[
            pltpu.VMEM((1, 1), i32),
            pltpu.VMEM((1, slots), i32),
            pltpu.VMEM((1, slots), i32),
            pltpu.VMEM(src_coords.shape, i32),
            pltpu.VMEM(tgt_coords.shape, i32),
            pltpu.VMEM(src_split, i32),
            pltpu.VMEM(tgt_block, i32),
            pltpu.VMEM(tgt_block, f32),
            pltpu.SemaphoreType.DMA((8,)),
            pltpu.VMEM((8, LANES), i32),
            pltpu.SMEM((8, LANES), i32),
            pltpu.SemaphoreType.DMA,
            pltpu.VMEM((slots, LANES), i32),
            pltpu.VMEM((slots, LANES), i32),
            pltpu.VMEM((src_tiles, 8, LANES), f32),
            pltpu.VMEM((src_tiles, 8, LANES), f32),
            pltpu.VMEM((tgt_tiles, 8, LANES), f32),
            pltpu.VMEM((tgt_tiles, 8, LANES), f32),
            pltpu.VMEM(src_block, f32),
            pltpu.VMEM(tgt_block, f32),
            pltpu.VMEM(src_split[1:], f32),
            pltpu.VMEM(tgt_block, f32),
            pltpu.VMEM((ITERS,) + src_split, f32),
            pltpu.VMEM((ITERS + 1,) + tgt_block, f32),
            pltpu.VMEM((slots, LANES), f32),
            pltpu.VMEM((slots, LANES), f32),
            pltpu.VMEM((slots + 8, LANES), f32),
            pltpu.VMEM(src_split, f32),
            pltpu.VMEM((ITERS,) + src_split, f32),
            pltpu.VMEM((ITERS, n_row) + tgt_block, f32),
            pltpu.VMEM((n_row, 8, LANES), f32),
            pltpu.VMEM((n_col, 8, LANES), f32),
            pltpu.SemaphoreType.DMA((2, n_row + n_col - 2)),
            pltpu.SemaphoreType.DMA((ITERS, 2, 2, n_col - 1)),
            pltpu.SemaphoreType.DMA((ITERS, 2, n_row - 1)),
        ],
        compiler_params=pltpu.CompilerParams(
            collective_id=0, has_side_effects=True, vmem_limit_bytes=56 * 1024 * 1024
        ),
        name="sinkhorn",
    )(
        kept_count, kept_src.reshape(1, slots), kept_tgt.reshape(1, slots),
        src_coords, tgt_coords,
        src_mass.reshape(src_split), tgt_mass.reshape(tgt_block), tgt_start.reshape(tgt_block),
    )
    return src_out.reshape(-1), tgt_out.reshape(-1)


def solution(mesh):
    placed = (
        P(None, "row"), P(None, "col"), P("row"), P("col"), P("col"),
        P("row", "col", None), P("row", "col", None), P("row", "col"),
    )
    return jax.shard_map(
        functools.partial(on_device, mesh.shape["row"], mesh.shape["col"]),
        mesh=mesh, in_specs=placed, out_specs=(P("row"), P("col")), check_vma=False,
    )
```

```python
import functools
import math

import jax
import jax.numpy as jnp
from jax import lax
from jax.experimental import pallas as pl
from jax.experimental.pallas import tpu as pltpu
from jax.sharding import PartitionSpec as P

ITERS = 3
LANES = 128
NEG = -1e30
CENTRE = 26.0
UNROLL = 16
MESH = pl.DeviceIdType.MESH

COST = 0.05
EXP2 = COST * math.log2(math.e)


def order_slots(ids, others, live, tiles):
    slots = ids.shape[1]
    lane = lax.broadcasted_iota(jnp.int32, (slots, slots), 1)
    sub = lax.broadcasted_iota(jnp.int32, (slots, slots), 0)

    def column(row):
        spread = jnp.broadcast_to(row, (slots, slots))
        return jnp.sum(jnp.where(lane == sub, spread, 0), axis=1, keepdims=True)

    key = jnp.where(live, ids, tiles) * slots + lane[0:1, :]
    mine = jnp.where(live, ids, tiles)
    key_col, mine_col = column(key), column(mine)
    before = (key < key_col).astype(jnp.int32)
    rank_col = jnp.sum(before, axis=1, keepdims=True)
    after = (key_col < key).astype(jnp.int32)
    rank = jnp.sum(after, axis=0, keepdims=True)
    hit = rank_col == lane
    sorted_ids = jnp.sum(jnp.where(hit, column(ids), 0), axis=0, keepdims=True)
    sorted_others = jnp.sum(jnp.where(hit, column(others), 0), axis=0, keepdims=True)
    earlier = (mine_col == mine) & (sub < lane)
    place = jnp.sum(earlier.astype(jnp.int32), axis=0, keepdims=True)
    place = jnp.where(live, place, -1)
    place = jnp.sum(
        jnp.where(rank == sub, jnp.broadcast_to(place, (slots, slots)), 0), axis=1, keepdims=True
    )
    tile = lax.broadcasted_iota(jnp.int32, (slots, LANES), 1)
    upto = jnp.sum((mine_col <= tile).astype(jnp.int32), axis=0, keepdims=True)
    held = jnp.sum((mine_col == tile).astype(jnp.int32), axis=0, keepdims=True)
    last = jnp.where(held > 0, upto - 1, slots)
    return sorted_ids, sorted_others, last, jnp.broadcast_to(place, (slots, LANES))


def offsets(n):
    return sorted(range(1, n), key=lambda off: abs(2 * off - n))


def kernel(
    n_row, n_col,
    count, kept_src, kept_tgt, src_xyz_in, tgt_xyz_in, src_mass_in, tgt_mass_in, start_in,
    src_out, tgt_out,
    live_count, src_ids, tgt_ids, src_xyz, tgt_xyz, src_mass, tgt_mass, start, load_sems,
    idx_rows, idx, idx_sem, place_s, place_t,
    a_src, b_src, a_tgt, b_tgt, sq_src, sq_tgt, log_src, log_tgt,
    hat_src, hat_tgt, peak, total, runs, send_src, got_src, got_tgt,
    mass_src, mass_tgt, mass_sems, src_sems, tgt_sems,
):
    row, col = lax.axis_index("row"), lax.axis_index("col")
    slots = place_s.shape[0]
    sublane = lax.broadcasted_iota(jnp.int32, (8, LANES), 0)

    loads = [
        pltpu.make_async_copy(src, dst, load_sems.at[k])
        for k, (src, dst) in enumerate((
            (kept_src, src_ids), (kept_tgt, tgt_ids), (src_mass_in, src_mass),
            (tgt_mass_in, tgt_mass), (src_xyz_in, src_xyz), (tgt_xyz_in, tgt_xyz),
            (start_in, start), (count, live_count),
        ))
    ]
    for load in loads:
        load.start()

    barrier = pltpu.get_barrier_semaphore()
    for axis, me, n in (("row", row, n_row), ("col", col, n_col)):
        for off in range(1, n):
            pl.semaphore_signal(
                barrier, inc=1, device_id={axis: lax.rem(me + off, n)}, device_id_type=MESH
            )

    for load in loads[:2] + loads[7:]:
        load.wait()
    live = lax.broadcasted_iota(jnp.int32, (1, slots), 1) < live_count[...]
    idx_rows[...] = jnp.zeros_like(idx_rows)
    for k, (ids, others, place, tiles) in enumerate((
        (src_ids, tgt_ids, place_s, a_src.shape[0]), (tgt_ids, src_ids, place_t, a_tgt.shape[0]),
    )):
        mine, theirs, last, place[...] = order_slots(ids[...], others[...], live, tiles)
        idx_rows[3 * k : 3 * k + 1, 0:slots] = mine
        idx_rows[3 * k + 1 : 3 * k + 2, 0:slots] = theirs
        idx_rows[3 * k + 2 : 3 * k + 3, :] = last
    to_scalars = pltpu.make_async_copy(idx_rows, idx, idx_sem)
    to_scalars.start()
    for load in loads[2:4]:
        load.wait()
    for mass, held, me in ((src_mass, mass_src, row), (tgt_mass, mass_tgt, col)):
        lane_sum = jnp.sum(
            mass[...].reshape(-1, LANES), axis=0, keepdims=True
        )
        held[me] = jnp.broadcast_to(lane_sum.astype(jnp.float32), (8, LANES))

    def set_up(xyz, a_ref, b_ref, sq_ref):
        def step(block, carry):
            for u in range(UNROLL):
                t = block * UNROLL + u
                at = pl.ds(pl.multiple_of(t * LANES, LANES), LANES)
                x, y, z = (xyz[d : d + 1, at].astype(jnp.float32) - CENTRE for d in range(3))
                sq_ref[pl.ds(t, 1), :] = x * x + y * y + z * z
                rows = jnp.where(
                    sublane == 0, x, jnp.where(sublane == 1, y, jnp.where(sublane == 2, z, 0.0))
                )
                a_ref[t] = rows
                b_ref[t] = jnp.where(sublane < 3, 2.0 * rows, jnp.where(sublane < 6, 1.0, 0.0))
            return carry

        lax.fori_loop(0, a_ref.shape[0] // UNROLL, step, 0)

    for load in loads[4:7]:
        load.wait()
    set_up(src_xyz, a_src, b_src, sq_src)
    set_up(tgt_xyz, a_tgt, b_tgt, sq_tgt)
    hat_tgt[0] = start[...] * (1.0 / COST) - sq_tgt[...]
    runs[pl.ds(slots, 8), :] = jnp.full((8, LANES), NEG, jnp.float32)

    pl.semaphore_wait(barrier, n_row + n_col - 2)

    mass_copies = []
    for axis, held, me, n, base in (
        ("row", mass_src, row, n_row, 0), ("col", mass_tgt, col, n_col, n_row - 1),
    ):
        for off in range(1, n):
            copy = pltpu.make_async_remote_copy(
                src_ref=held.at[me], dst_ref=held.at[me],
                send_sem=mass_sems.at[0, base + off - 1], recv_sem=mass_sems.at[1, base + off - 1],
                device_id={axis: lax.rem(me + off, n)}, device_id_type=MESH,
            )
            copy.start()
            mass_copies.append(copy)
    to_scalars.wait()

    def join(joined, top, summed, top_before, sum_before):
        both = jnp.maximum(top, top_before)
        low = jnp.exp2((jnp.minimum(top, top_before) - both) * EXP2)
        here = top >= top_before
        both_sum = jnp.where(here, summed, sum_before) + low * jnp.where(
            here, sum_before, summed
        )
        return jnp.where(joined, both, top), jnp.where(joined, both_sum, summed)

    def merge_runs(first, place, carried):
        rows = slice(first, first + 8)
        place, top, summed = place[rows, :], peak[rows, :], total[rows, :]
        for reach in (1, 2, 4):
            top, summed = join(
                (place >= reach) & (sublane >= reach), top, summed,
                pltpu.roll(top, reach, axis=0), pltpu.roll(summed, reach, axis=0),
            )
        if carried is not None:
            top, summed = join(place > sublane, top, summed, *carried)
        runs[rows, :] = jnp.where(place >= 0, top * COST + jnp.log(summed), NEG)
        return tuple(jnp.broadcast_to(x[7:8, :], (8, LANES)) for x in (top, summed))

    def partials(load_hat, a_ref, b_ref, in_row, out_row, place):
        carried = None
        for u in range(0, slots, 2):
            lefts, rights = [], []
            for v in range(2):
                p = u + v
                i_in, i_out = idx[in_row, p], idx[out_row, p]
                hat = jnp.broadcast_to(load_hat(i_in), (8, LANES))
                high = hat.astype(jnp.bfloat16).astype(jnp.float32)
                rest = hat - high
                mid = rest.astype(jnp.bfloat16).astype(jnp.float32)
                low = rest - mid
                lefts.append(jnp.where(
                    sublane == 3, high,
                    jnp.where(sublane == 4, mid, jnp.where(sublane == 5, low, a_ref[i_in])),
                ))
                zero = jnp.zeros((8, LANES), jnp.float32)
                pair = [b_ref[i_out], zero] if v == 0 else [zero, b_ref[i_out]]
                rights.append(jnp.concatenate(pair, axis=1))
            scores = lax.dot_general(
                jnp.concatenate(lefts, axis=0).astype(jnp.bfloat16),
                jnp.concatenate(rights, axis=0).astype(jnp.bfloat16),
                (((0,), (0,)), ((), ())), preferred_element_type=jnp.float32,
            )
            for v in range(2):
                p = u + v
                part = scores[:, v * LANES : (v + 1) * LANES]
                top = jnp.max(part, axis=0, keepdims=True)
                peak[pl.ds(p, 1), :] = top
                total[pl.ds(p, 1), :] = jnp.sum(
                    jnp.exp2((part - top) * EXP2), axis=0, keepdims=True
                )
            if u % 8 == 6:
                carried = merge_runs(u - 6, place, carried)

    def send(axis, me, n, off, src, dst, sems):
        copy = pltpu.make_async_remote_copy(
            src_ref=src, dst_ref=dst, send_sem=sems.at[0, off - 1], recv_sem=sems.at[1, off - 1],
            device_id={axis: lax.rem(me + off, n)}, device_id_type=MESH,
        )
        copy.start()
        return copy

    def merged(parts):
        top = functools.reduce(jnp.maximum, parts)
        return top + jnp.log(functools.reduce(jnp.add, [jnp.exp(part - top) for part in parts]))

    def mass_logs():
        for copy in mass_copies:
            copy.wait()
        src_all = jnp.sum(jnp.sum(mass_src[...], axis=0)[0:1, :], axis=1, keepdims=True)
        tgt_all = jnp.sum(jnp.sum(mass_tgt[...], axis=0)[0:1, :], axis=1, keepdims=True)
        log_src[...] = jnp.log(src_mass[col].astype(jnp.float32)) - jnp.log(src_all)
        log_tgt[...] = jnp.log(tgt_mass[...].astype(jnp.float32)) - jnp.log(tgt_all)

    def merge_src(it):
        tp = send_src.shape[1]
        first = []
        for off in offsets(n_col) + [0]:
            peer = lax.rem(col + off, n_col)
            for u in range(tp):
                send_src[peer, u : u + 1, :] = runs[pl.ds(idx[2, peer * tp + u], 1), :]
            if off > 0:
                first.append(send(
                    "col", col, n_col, off,
                    send_src.at[peer], got_src.at[it, col], src_sems.at[it, 0],
                ))
        pl.when(it == 0)(mass_logs)
        for copy in first:
            copy.wait_recv()
        parts = [send_src[col]] + [
            got_src[it, lax.rem(col + off, n_col)] for off in range(1, n_col)
        ]
        hat_src[it, col] = (log_src[...] - merged(parts)) * (1.0 / COST)
        mine = hat_src.at[it, col]
        second = [
            send("col", col, n_col, off, mine, mine, src_sems.at[it, 1])
            for off in offsets(n_col)
        ]
        for copy in second:
            copy.wait_recv()
        return first + second

    def merge_tgt(it):
        for t in range(got_tgt.shape[2]):
            got_tgt[it, row, t : t + 1, :] = runs[pl.ds(idx[5, t], 1), :]
        mine = got_tgt.at[it, row]
        copies = [
            send("row", row, n_row, off, mine, mine, tgt_sems.at[it]) for off in offsets(n_row)
        ]
        @pl.when(it == ITERS - 1)
        def _():
            src_hat = hat_src[ITERS - 1].reshape(sq_src.shape)
            src_out[...] = (src_hat + sq_src[...]) * COST

        for copy in copies:
            copy.wait_recv()
        parts = [got_tgt[it, r] for r in range(n_row)]
        hat_tgt[it + 1] = (log_tgt[...] - merged(parts)) * (1.0 / COST)
        for copy in copies:
            copy.wait_send()

    def iterate(it, carry):
        partials(lambda t: hat_tgt[it, pl.ds(t, 1), :], a_tgt, b_src, 1, 0, place_s)
        sent = merge_src(it)
        tp = hat_src.shape[2]
        partials(
            lambda t: hat_src[it, t // tp, pl.ds(t % tp, 1), :], a_src, b_tgt, 4, 3, place_t
        )
        for copy in sent:
            copy.wait_send()
        merge_tgt(it)
        return carry

    lax.fori_loop(0, ITERS, iterate, 0)
    tgt_out[...] = (hat_tgt[ITERS] + sq_tgt[...]) * COST


def on_device(
    n_row, n_col,
    src_coords, tgt_coords, src_mass, tgt_mass, tgt_start, kept_src, kept_tgt, kept_count,
):
    slots = kept_src.shape[-1]
    src_tiles, tgt_tiles = src_coords.shape[1] // LANES, tgt_coords.shape[1] // LANES
    src_split = (n_col, src_tiles // n_col, LANES)
    src_block, tgt_block = (src_tiles, LANES), (tgt_tiles, LANES)
    f32, i32 = jnp.float32, jnp.int32
    src_out, tgt_out = pl.pallas_call(
        functools.partial(kernel, n_row, n_col),
        out_shape=(
            jax.ShapeDtypeStruct(src_block, f32),
            jax.ShapeDtypeStruct(tgt_block, f32),
        ),
        in_specs=[pl.BlockSpec(memory_space=pl.ANY)] * 8,
        out_specs=(pl.BlockSpec(memory_space=pltpu.VMEM),) * 2,
        scratch_shapes=[
            pltpu.VMEM((1, 1), i32),
            pltpu.VMEM((1, slots), i32),
            pltpu.VMEM((1, slots), i32),
            pltpu.VMEM(src_coords.shape, i32),
            pltpu.VMEM(tgt_coords.shape, i32),
            pltpu.VMEM(src_split, i32),
            pltpu.VMEM(tgt_block, i32),
            pltpu.VMEM(tgt_block, f32),
            pltpu.SemaphoreType.DMA((8,)),
            pltpu.VMEM((8, LANES), i32),
            pltpu.SMEM((8, LANES), i32),
            pltpu.SemaphoreType.DMA,
            pltpu.VMEM((slots, LANES), i32),
            pltpu.VMEM((slots, LANES), i32),
            pltpu.VMEM((src_tiles, 8, LANES), f32),
            pltpu.VMEM((src_tiles, 8, LANES), f32),
            pltpu.VMEM((tgt_tiles, 8, LANES), f32),
            pltpu.VMEM((tgt_tiles, 8, LANES), f32),
            pltpu.VMEM(src_block, f32),
            pltpu.VMEM(tgt_block, f32),
            pltpu.VMEM(src_split[1:], f32),
            pltpu.VMEM(tgt_block, f32),
            pltpu.VMEM((ITERS,) + src_split, f32),
            pltpu.VMEM((ITERS + 1,) + tgt_block, f32),
            pltpu.VMEM((slots, LANES), f32),
            pltpu.VMEM((slots, LANES), f32),
            pltpu.VMEM((slots + 8, LANES), f32),
            pltpu.VMEM(src_split, f32),
            pltpu.VMEM((ITERS,) + src_split, f32),
            pltpu.VMEM((ITERS, n_row) + tgt_block, f32),
            pltpu.VMEM((n_row, 8, LANES), f32),
            pltpu.VMEM((n_col, 8, LANES), f32),
            pltpu.SemaphoreType.DMA((2, n_row + n_col - 2)),
            pltpu.SemaphoreType.DMA((ITERS, 2, 2, n_col - 1)),
            pltpu.SemaphoreType.DMA((ITERS, 2, n_row - 1)),
        ],
        compiler_params=pltpu.CompilerParams(
            collective_id=0, has_side_effects=True, vmem_limit_bytes=56 * 1024 * 1024
        ),
        name="sinkhorn",
    )(
        kept_count, kept_src.reshape(1, slots), kept_tgt.reshape(1, slots),
        src_coords, tgt_coords,
        src_mass.reshape(src_split), tgt_mass.reshape(tgt_block), tgt_start.reshape(tgt_block),
    )
    return src_out.reshape(-1), tgt_out.reshape(-1)


def solution(mesh):
    placed = (
        P(None, "row"), P(None, "col"), P("row"), P("col"), P("col"),
        P("row", "col", None), P("row", "col", None), P("row", "col"),
    )
    return jax.shard_map(
        functools.partial(on_device, mesh.shape["row"], mesh.shape["col"]),
        mesh=mesh, in_specs=placed, out_specs=(P("row"), P("col")), check_vma=False,
    )
```

```python
import functools
import math

import jax
import jax.numpy as jnp
from jax import lax
from jax.experimental import pallas as pl
from jax.experimental.pallas import tpu as pltpu
from jax.sharding import PartitionSpec as P

ITERS = 3
LANES = 128
NEG = -1e30
CENTRE = 26.0
UNROLL = 16
MESH = pl.DeviceIdType.MESH

COST = 0.05
EXP2 = COST * math.log2(math.e)


def order_slots(first, second, live, first_tiles, second_tiles):
    slots = first.shape[1]
    lane = lax.broadcasted_iota(jnp.int32, (slots, slots), 1)
    sub = lax.broadcasted_iota(jnp.int32, (slots, slots), 0)
    tile = lax.broadcasted_iota(jnp.int32, (slots, LANES), 1)

    def column(row):
        return jnp.broadcast_to(row, (slots, slots)).T

    def count(hits):
        return jnp.sum(jnp.where(hits, 1, 0), axis=0, keepdims=True)

    sides = []
    for ids, tiles in ((first, first_tiles), (second, second_tiles)):
        mine = jnp.where(live, ids, tiles)
        mine_col = column(mine)
        sides.append((mine, mine_col, jnp.where(mine_col == tiles, 0, mine_col)))
    out = []
    for (mine, mine_col, ids_col), other in ((sides[0], sides[1]), (sides[1], sides[0])):
        earlier = (mine_col == mine) & (sub < lane)
        rank = count((mine_col < mine) | earlier)
        hit = column(rank) == lane
        place = jnp.where(live, count(earlier), -1)
        sorted_ids = jnp.sum(jnp.where(hit, ids_col, 0), axis=0, keepdims=True)
        sorted_others = jnp.sum(jnp.where(hit, other[2], 0), axis=0, keepdims=True)
        sorted_place = jnp.sum(jnp.where(hit, column(place), 0), axis=0, keepdims=True)
        place_col = column(sorted_place)[:, 0:1]
        held = mine_col[:, 0:1]
        last = jnp.where(count(held == tile) > 0, count(held <= tile) - 1, slots)
        out.append((sorted_ids, sorted_others, last, jnp.broadcast_to(place_col, (slots, LANES))))
    return out


def kernel(
    n_row, n_col,
    count, kept_src, kept_tgt, src_xyz_in, tgt_xyz_in, src_mass_in, tgt_mass_in, start_in,
    src_out, tgt_out,
    live_count, src_ids, tgt_ids, src_xyz, tgt_xyz, src_mass, tgt_mass, start, load_sems,
    idx_rows, idx, idx_sem, place_s, place_t,
    a_src, b_src, a_tgt, b_tgt, sq_src, sq_tgt, log_src, log_tgt,
    hat_src, hat_tgt, peak, total, runs, send_src, got_src, got_tgt,
    mass_src, mass_tgt, mass_sems, src_sems, tgt_sems,
):
    row, col = lax.axis_index("row"), lax.axis_index("col")
    slots = place_s.shape[0]
    sublane = lax.broadcasted_iota(jnp.int32, (8, LANES), 0)

    loads = [
        pltpu.make_async_copy(src, dst, load_sems.at[k])
        for k, (src, dst) in enumerate((
            (kept_src, src_ids), (kept_tgt, tgt_ids), (src_mass_in, src_mass),
            (tgt_mass_in, tgt_mass), (src_xyz_in, src_xyz), (tgt_xyz_in, tgt_xyz),
            (start_in, start), (count, live_count),
        ))
    ]
    for load in loads:
        load.start()

    barrier = pltpu.get_barrier_semaphore()
    for axis, me, n in (("row", row, n_row), ("col", col, n_col)):
        for off in range(1, n):
            pl.semaphore_signal(
                barrier, inc=1, device_id={axis: lax.rem(me + off, n)}, device_id_type=MESH
            )

    for load in loads[:2] + loads[7:]:
        load.wait()
    live = lax.broadcasted_iota(jnp.int32, (1, slots), 1) < live_count[...]
    idx_rows[...] = jnp.zeros_like(idx_rows)
    orders = order_slots(src_ids[...], tgt_ids[...], live, a_src.shape[0], a_tgt.shape[0])
    for k, (order, place) in enumerate(zip(orders, (place_s, place_t))):
        mine, theirs, last, place[...] = order
        idx_rows[3 * k : 3 * k + 1, 0:slots] = mine
        idx_rows[3 * k + 1 : 3 * k + 2, 0:slots] = theirs
        idx_rows[3 * k + 2 : 3 * k + 3, :] = last
    to_scalars = pltpu.make_async_copy(idx_rows, idx, idx_sem)
    to_scalars.start()
    for load in loads[2:4]:
        load.wait()
    for mass, held, me in ((src_mass, mass_src, row), (tgt_mass, mass_tgt, col)):
        lane_sum = jnp.sum(
            mass[...].reshape(-1, LANES), axis=0, keepdims=True
        )
        held[me] = jnp.broadcast_to(lane_sum.astype(jnp.float32), (8, LANES))

    def set_up(xyz, a_ref, b_ref, sq_ref):
        def step(block, carry):
            for u in range(UNROLL):
                t = block * UNROLL + u
                at = pl.ds(pl.multiple_of(t * LANES, LANES), LANES)
                x, y, z = (xyz[d : d + 1, at].astype(jnp.float32) - CENTRE for d in range(3))
                sq_ref[pl.ds(t, 1), :] = x * x + y * y + z * z
                rows = jnp.where(
                    sublane == 0, x, jnp.where(sublane == 1, y, jnp.where(sublane == 2, z, 0.0))
                )
                a_ref[t] = rows
                b_ref[t] = jnp.where(sublane < 3, 2.0 * rows, jnp.where(sublane < 6, 1.0, 0.0))
            return carry

        lax.fori_loop(0, a_ref.shape[0] // UNROLL, step, 0)

    for load in loads[4:7]:
        load.wait()
    set_up(src_xyz, a_src, b_src, sq_src)
    set_up(tgt_xyz, a_tgt, b_tgt, sq_tgt)
    hat_tgt[0] = start[...] * (1.0 / COST) - sq_tgt[...]
    runs[pl.ds(slots, 8), :] = jnp.full((8, LANES), NEG, jnp.float32)

    pl.semaphore_wait(barrier, n_row + n_col - 2)

    mass_copies = []
    for axis, held, me, n, base in (
        ("row", mass_src, row, n_row, 0), ("col", mass_tgt, col, n_col, n_row - 1),
    ):
        for off in range(1, n):
            copy = pltpu.make_async_remote_copy(
                src_ref=held.at[me], dst_ref=held.at[me],
                send_sem=mass_sems.at[0, base + off - 1], recv_sem=mass_sems.at[1, base + off - 1],
                device_id={axis: lax.rem(me + off, n)}, device_id_type=MESH,
            )
            copy.start()
            mass_copies.append(copy)
    to_scalars.wait()

    def partials(load_hat, a_ref, b_ref, in_row, out_row, place):
        for u in range(0, slots, 2):
            lefts, rights = [], []
            for v in range(2):
                p = u + v
                i_in, i_out = idx[in_row, p], idx[out_row, p]
                hat = jnp.broadcast_to(load_hat(i_in), (8, LANES))
                high = hat.astype(jnp.bfloat16).astype(jnp.float32)
                rest = hat - high
                mid = rest.astype(jnp.bfloat16).astype(jnp.float32)
                low = rest - mid
                lefts.append(jnp.where(
                    sublane == 3, high,
                    jnp.where(sublane == 4, mid, jnp.where(sublane == 5, low, a_ref[i_in])),
                ))
                zero = jnp.zeros((8, LANES), jnp.float32)
                pair = [b_ref[i_out], zero] if v == 0 else [zero, b_ref[i_out]]
                rights.append(jnp.concatenate(pair, axis=1))
            scores = lax.dot_general(
                jnp.concatenate(lefts, axis=0).astype(jnp.bfloat16),
                jnp.concatenate(rights, axis=0).astype(jnp.bfloat16),
                (((0,), (0,)), ((), ())), preferred_element_type=jnp.float32,
            )
            for v in range(2):
                p = u + v
                part = scores[:, v * LANES : (v + 1) * LANES]
                top = jnp.max(part, axis=0, keepdims=True)
                peak[pl.ds(p, 1), :] = top
                total[pl.ds(p, 1), :] = jnp.sum(
                    jnp.exp2((part - top) * EXP2), axis=0, keepdims=True
                )
        where_in = place[...]
        top, summed = peak[...], total[...]
        reach = 1
        while reach < slots:
            top_before = pltpu.roll(top, reach, axis=0)
            sum_before = pltpu.roll(summed, reach, axis=0)
            both = jnp.maximum(top, top_before)
            low = jnp.exp2((jnp.minimum(top, top_before) - both) * EXP2)
            here = top >= top_before
            both_sum = jnp.where(here, summed, sum_before) + low * jnp.where(
                here, sum_before, summed
            )
            joined = where_in >= reach
            top, summed = jnp.where(joined, both, top), jnp.where(joined, both_sum, summed)
            reach *= 2
        runs[pl.ds(0, slots), :] = jnp.where(
            where_in >= 0, top * COST + jnp.log(summed), NEG
        )

    def send(axis, me, n, off, src, dst, sems):
        copy = pltpu.make_async_remote_copy(
            src_ref=src, dst_ref=dst, send_sem=sems.at[0, off - 1], recv_sem=sems.at[1, off - 1],
            device_id={axis: lax.rem(me + off, n)}, device_id_type=MESH,
        )
        copy.start()
        return copy

    def merged(parts):
        top = functools.reduce(jnp.maximum, parts)
        return top + jnp.log(functools.reduce(jnp.add, [jnp.exp(part - top) for part in parts]))

    def mass_logs():
        for copy in mass_copies:
            copy.wait()
        src_all = jnp.sum(jnp.sum(mass_src[...], axis=0)[0:1, :], axis=1, keepdims=True)
        tgt_all = jnp.sum(jnp.sum(mass_tgt[...], axis=0)[0:1, :], axis=1, keepdims=True)
        log_src[...] = jnp.log(src_mass[col].astype(jnp.float32)) - jnp.log(src_all)
        log_tgt[...] = jnp.log(tgt_mass[...].astype(jnp.float32)) - jnp.log(tgt_all)

    def merge_src(it):
        tp = send_src.shape[1]
        first = []
        for off in range(n_col):
            peer = lax.rem(col + 1 + off, n_col)
            for u in range(tp):
                send_src[peer, u : u + 1, :] = runs[pl.ds(idx[2, peer * tp + u], 1), :]
            if off < n_col - 1:
                first.append(send(
                    "col", col, n_col, off + 1,
                    send_src.at[peer], got_src.at[it, col], src_sems.at[it, 0],
                ))
        pl.when(it == 0)(mass_logs)
        for copy in first:
            copy.wait_recv()
        parts = [send_src[col]] + [
            got_src[it, lax.rem(col + off, n_col)] for off in range(1, n_col)
        ]
        hat_src[it, col] = (log_src[...] - merged(parts)) * (1.0 / COST)
        mine = hat_src.at[it, col]
        second = [
            send("col", col, n_col, off, mine, mine, src_sems.at[it, 1])
            for off in range(1, n_col)
        ]
        for copy in second:
            copy.wait_recv()
        for copy in first + second:
            copy.wait_send()

    def merge_tgt(it):
        tiles = got_tgt.shape[2]

        def pick(block, carry):
            for u in range(UNROLL):
                t = block * UNROLL + u
                got_tgt[it, row, pl.ds(t, 1), :] = runs[pl.ds(idx[5, t], 1), :]
            return carry

        lax.fori_loop(0, tiles // UNROLL, pick, 0)
        mine = got_tgt.at[it, row]
        copies = [
            send("row", row, n_row, off, mine, mine, tgt_sems.at[it]) for off in range(1, n_row)
        ]
        @pl.when(it == ITERS - 1)
        def _():
            src_hat = hat_src[ITERS - 1].reshape(sq_src.shape)
            src_out[...] = (src_hat + sq_src[...]) * COST

        for copy in copies:
            copy.wait()
        parts = [got_tgt[it, r] for r in range(n_row)]
        hat_tgt[it + 1] = (log_tgt[...] - merged(parts)) * (1.0 / COST)

    def iterate(it, carry):
        partials(lambda t: hat_tgt[it, pl.ds(t, 1), :], a_tgt, b_src, 1, 0, place_s)
        merge_src(it)
        tp = hat_src.shape[2]
        partials(
            lambda t: hat_src[it, t // tp, pl.ds(t % tp, 1), :], a_src, b_tgt, 4, 3, place_t
        )
        merge_tgt(it)
        return carry

    lax.fori_loop(0, ITERS, iterate, 0)
    tgt_out[...] = (hat_tgt[ITERS] + sq_tgt[...]) * COST


def on_device(
    n_row, n_col,
    src_coords, tgt_coords, src_mass, tgt_mass, tgt_start, kept_src, kept_tgt, kept_count,
):
    slots = kept_src.shape[-1]
    src_tiles, tgt_tiles = src_coords.shape[1] // LANES, tgt_coords.shape[1] // LANES
    src_split = (n_col, src_tiles // n_col, LANES)
    src_block, tgt_block = (src_tiles, LANES), (tgt_tiles, LANES)
    f32, i32 = jnp.float32, jnp.int32
    src_out, tgt_out = pl.pallas_call(
        functools.partial(kernel, n_row, n_col),
        out_shape=(
            jax.ShapeDtypeStruct(src_block, f32),
            jax.ShapeDtypeStruct(tgt_block, f32),
        ),
        in_specs=[pl.BlockSpec(memory_space=pl.ANY)] * 8,
        out_specs=(pl.BlockSpec(memory_space=pltpu.VMEM),) * 2,
        scratch_shapes=[
            pltpu.VMEM((1, 1), i32),
            pltpu.VMEM((1, slots), i32),
            pltpu.VMEM((1, slots), i32),
            pltpu.VMEM(src_coords.shape, i32),
            pltpu.VMEM(tgt_coords.shape, i32),
            pltpu.VMEM(src_split, i32),
            pltpu.VMEM(tgt_block, i32),
            pltpu.VMEM(tgt_block, f32),
            pltpu.SemaphoreType.DMA((8,)),
            pltpu.VMEM((8, LANES), i32),
            pltpu.SMEM((8, LANES), i32),
            pltpu.SemaphoreType.DMA,
            pltpu.VMEM((slots, LANES), i32),
            pltpu.VMEM((slots, LANES), i32),
            pltpu.VMEM((src_tiles, 8, LANES), f32),
            pltpu.VMEM((src_tiles, 8, LANES), f32),
            pltpu.VMEM((tgt_tiles, 8, LANES), f32),
            pltpu.VMEM((tgt_tiles, 8, LANES), f32),
            pltpu.VMEM(src_block, f32),
            pltpu.VMEM(tgt_block, f32),
            pltpu.VMEM(src_split[1:], f32),
            pltpu.VMEM(tgt_block, f32),
            pltpu.VMEM((ITERS,) + src_split, f32),
            pltpu.VMEM((ITERS + 1,) + tgt_block, f32),
            pltpu.VMEM((slots, LANES), f32),
            pltpu.VMEM((slots, LANES), f32),
            pltpu.VMEM((slots + 8, LANES), f32),
            pltpu.VMEM(src_split, f32),
            pltpu.VMEM((ITERS,) + src_split, f32),
            pltpu.VMEM((ITERS, n_row) + tgt_block, f32),
            pltpu.VMEM((n_row, 8, LANES), f32),
            pltpu.VMEM((n_col, 8, LANES), f32),
            pltpu.SemaphoreType.DMA((2, n_row + n_col - 2)),
            pltpu.SemaphoreType.DMA((ITERS, 2, 2, n_col - 1)),
            pltpu.SemaphoreType.DMA((ITERS, 2, n_row - 1)),
        ],
        compiler_params=pltpu.CompilerParams(
            collective_id=0, has_side_effects=True, vmem_limit_bytes=56 * 1024 * 1024
        ),
        name="sinkhorn",
    )(
        kept_count, kept_src.reshape(1, slots), kept_tgt.reshape(1, slots),
        src_coords, tgt_coords,
        src_mass.reshape(src_split), tgt_mass.reshape(tgt_block), tgt_start.reshape(tgt_block),
    )
    return src_out.reshape(-1), tgt_out.reshape(-1)


def solution(mesh):
    placed = (
        P(None, "row"), P(None, "col"), P("row"), P("col"), P("col"),
        P("row", "col", None), P("row", "col", None), P("row", "col"),
    )
    return jax.shard_map(
        functools.partial(on_device, mesh.shape["row"], mesh.shape["col"]),
        mesh=mesh, in_specs=placed, out_specs=(P("row"), P("col")), check_vma=False,
    )
```

```python
import functools
import math

import jax
import jax.numpy as jnp
from jax import lax
from jax.experimental import pallas as pl
from jax.experimental.pallas import tpu as pltpu
from jax.sharding import PartitionSpec as P

ITERS = 3
LANES = 128
NEG = -1e30
CENTRE = 26.0
UNROLL = 16
MESH = pl.DeviceIdType.MESH

COST = 0.05
EXP2 = COST * math.log2(math.e)


def order_slots(first, second, live, first_tiles, second_tiles):
    slots = first.shape[1]
    lane = lax.broadcasted_iota(jnp.int32, (slots, slots), 1)
    sub = lax.broadcasted_iota(jnp.int32, (slots, slots), 0)
    tile = lax.broadcasted_iota(jnp.int32, (slots, LANES), 1)

    def column(row):
        return jnp.broadcast_to(row, (slots, slots)).T

    def count(hits):
        return jnp.sum(jnp.where(hits, 1, 0), axis=0, keepdims=True)

    sides = []
    for ids, tiles in ((first, first_tiles), (second, second_tiles)):
        mine = jnp.where(live, ids, tiles)
        mine_col = column(mine)
        sides.append((mine, mine_col, jnp.where(mine_col == tiles, 0, mine_col)))
    out = []
    for (mine, mine_col, ids_col), other in ((sides[0], sides[1]), (sides[1], sides[0])):
        earlier = (mine_col == mine) & (sub < lane)
        rank = count((mine_col < mine) | earlier)
        hit = column(rank) == lane
        place = jnp.where(live, count(earlier), -1)
        sorted_ids = jnp.sum(jnp.where(hit, ids_col, 0), axis=0, keepdims=True)
        sorted_others = jnp.sum(jnp.where(hit, other[2], 0), axis=0, keepdims=True)
        sorted_place = jnp.sum(jnp.where(hit, column(place), 0), axis=0, keepdims=True)
        place_col = column(sorted_place)[:, 0:1]
        held = mine_col[:, 0:1]
        last = jnp.where(count(held == tile) > 0, count(held <= tile) - 1, slots)
        out.append((sorted_ids, sorted_others, last, jnp.broadcast_to(place_col, (slots, LANES))))
    return out


def kernel(
    n_row, n_col,
    count, kept_src, kept_tgt, src_xyz_in, tgt_xyz_in, src_mass_in, tgt_mass_in, start_in,
    src_out, tgt_out,
    live_count, src_ids, tgt_ids, src_xyz, tgt_xyz, src_mass, tgt_mass, start, load_sems,
    idx_rows, idx, idx_sem, place_s, place_t,
    a_src, b_src, a_tgt, b_tgt, sq_src, sq_tgt, log_src, log_tgt,
    hat_src, hat_tgt, peak, total, runs, send_src, got_src, got_tgt,
    mass_src, mass_tgt, mass_sems, src_sems, tgt_sems,
):
    row, col = lax.axis_index("row"), lax.axis_index("col")
    slots = place_s.shape[0]
    sublane = lax.broadcasted_iota(jnp.int32, (8, LANES), 0)

    loads = [
        pltpu.make_async_copy(src, dst, load_sems.at[k])
        for k, (src, dst) in enumerate((
            (kept_src, src_ids), (kept_tgt, tgt_ids), (src_mass_in, src_mass),
            (tgt_mass_in, tgt_mass), (src_xyz_in, src_xyz), (tgt_xyz_in, tgt_xyz),
            (start_in, start), (count, live_count),
        ))
    ]
    for load in loads:
        load.start()

    barrier = pltpu.get_barrier_semaphore()
    for axis, me, n in (("row", row, n_row), ("col", col, n_col)):
        for off in range(1, n):
            pl.semaphore_signal(
                barrier, inc=1, device_id={axis: lax.rem(me + off, n)}, device_id_type=MESH
            )

    for load in loads[:2] + loads[7:]:
        load.wait()
    live = lax.broadcasted_iota(jnp.int32, (1, slots), 1) < live_count[...]
    idx_rows[...] = jnp.zeros_like(idx_rows)
    orders = order_slots(src_ids[...], tgt_ids[...], live, a_src.shape[0], a_tgt.shape[0])
    for k, (order, place) in enumerate(zip(orders, (place_s, place_t))):
        mine, theirs, last, place[...] = order
        idx_rows[3 * k : 3 * k + 1, 0:slots] = mine
        idx_rows[3 * k + 1 : 3 * k + 2, 0:slots] = theirs
        idx_rows[3 * k + 2 : 3 * k + 3, :] = last
    to_scalars = pltpu.make_async_copy(idx_rows, idx, idx_sem)
    to_scalars.start()
    for load in loads[2:4]:
        load.wait()
    for mass, held, me in ((src_mass, mass_src, row), (tgt_mass, mass_tgt, col)):
        lane_sum = jnp.sum(
            mass[...].reshape(-1, LANES), axis=0, keepdims=True
        )
        held[me] = jnp.broadcast_to(lane_sum.astype(jnp.float32), (8, LANES))

    def set_up(xyz, a_ref, b_ref, sq_ref):
        def step(block, carry):
            for u in range(UNROLL):
                t = block * UNROLL + u
                at = pl.ds(pl.multiple_of(t * LANES, LANES), LANES)
                x, y, z = (xyz[d : d + 1, at].astype(jnp.float32) - CENTRE for d in range(3))
                sq_ref[pl.ds(t, 1), :] = x * x + y * y + z * z
                rows = jnp.where(
                    sublane == 0, x, jnp.where(sublane == 1, y, jnp.where(sublane == 2, z, 0.0))
                )
                a_ref[t] = rows
                b_ref[t] = jnp.where(sublane < 3, 2.0 * rows, jnp.where(sublane < 6, 1.0, 0.0))
            return carry

        lax.fori_loop(0, a_ref.shape[0] // UNROLL, step, 0)

    for load in loads[4:7]:
        load.wait()
    set_up(src_xyz, a_src, b_src, sq_src)
    set_up(tgt_xyz, a_tgt, b_tgt, sq_tgt)
    hat_tgt[0] = start[...] * (1.0 / COST) - sq_tgt[...]
    runs[pl.ds(slots, 8), :] = jnp.full((8, LANES), NEG, jnp.float32)

    pl.semaphore_wait(barrier, n_row + n_col - 2)

    mass_copies = []
    for axis, held, me, n, base in (
        ("row", mass_src, row, n_row, 0), ("col", mass_tgt, col, n_col, n_row - 1),
    ):
        for off in range(1, n):
            copy = pltpu.make_async_remote_copy(
                src_ref=held.at[me], dst_ref=held.at[me],
                send_sem=mass_sems.at[0, base + off - 1], recv_sem=mass_sems.at[1, base + off - 1],
                device_id={axis: lax.rem(me + off, n)}, device_id_type=MESH,
            )
            copy.start()
            mass_copies.append(copy)
    to_scalars.wait()

    def partials(load_hat, a_ref, b_ref, in_row, out_row, place):
        for u in range(0, slots, 2):
            lefts, rights = [], []
            for v in range(2):
                p = u + v
                i_in, i_out = idx[in_row, p], idx[out_row, p]
                hat = jnp.broadcast_to(load_hat(i_in), (8, LANES))
                high = hat.astype(jnp.bfloat16).astype(jnp.float32)
                rest = hat - high
                mid = rest.astype(jnp.bfloat16).astype(jnp.float32)
                low = rest - mid
                lefts.append(jnp.where(
                    sublane == 3, high,
                    jnp.where(sublane == 4, mid, jnp.where(sublane == 5, low, a_ref[i_in])),
                ))
                zero = jnp.zeros((8, LANES), jnp.float32)
                pair = [b_ref[i_out], zero] if v == 0 else [zero, b_ref[i_out]]
                rights.append(jnp.concatenate(pair, axis=1))
            scores = lax.dot_general(
                jnp.concatenate(lefts, axis=0).astype(jnp.bfloat16),
                jnp.concatenate(rights, axis=0).astype(jnp.bfloat16),
                (((0,), (0,)), ((), ())), preferred_element_type=jnp.float32,
            )
            for v in range(2):
                p = u + v
                part = scores[:, v * LANES : (v + 1) * LANES]
                part = part.reshape(LANES // 8, 8, LANES)
                tops = jnp.max(part, axis=0)
                sums = jnp.sum(jnp.exp2((part - tops) * EXP2), axis=0)
                top = jnp.max(tops, axis=0, keepdims=True)
                peak[pl.ds(p, 1), :] = top
                total[pl.ds(p, 1), :] = jnp.sum(
                    sums * jnp.exp2((tops - top) * EXP2), axis=0, keepdims=True
                )
        where_in = place[...]
        top, summed = peak[...], total[...]
        reach = 1
        while reach < slots:
            top_before = pltpu.roll(top, reach, axis=0)
            sum_before = pltpu.roll(summed, reach, axis=0)
            both = jnp.maximum(top, top_before)
            low = jnp.exp2((jnp.minimum(top, top_before) - both) * EXP2)
            here = top >= top_before
            both_sum = jnp.where(here, summed, sum_before) + low * jnp.where(
                here, sum_before, summed
            )
            joined = where_in >= reach
            top, summed = jnp.where(joined, both, top), jnp.where(joined, both_sum, summed)
            reach *= 2
        runs[pl.ds(0, slots), :] = jnp.where(
            where_in >= 0, top * COST + jnp.log(summed), NEG
        )

    def send(axis, me, n, off, src, dst, sems):
        copy = pltpu.make_async_remote_copy(
            src_ref=src, dst_ref=dst, send_sem=sems.at[0, off - 1], recv_sem=sems.at[1, off - 1],
            device_id={axis: lax.rem(me + off, n)}, device_id_type=MESH,
        )
        copy.start()
        return copy

    def merged(parts):
        top = functools.reduce(jnp.maximum, parts)
        return top + jnp.log(functools.reduce(jnp.add, [jnp.exp(part - top) for part in parts]))

    def mass_logs():
        for copy in mass_copies:
            copy.wait()
        src_all = jnp.sum(jnp.sum(mass_src[...], axis=0)[0:1, :], axis=1, keepdims=True)
        tgt_all = jnp.sum(jnp.sum(mass_tgt[...], axis=0)[0:1, :], axis=1, keepdims=True)
        log_src[...] = jnp.log(src_mass[col].astype(jnp.float32)) - jnp.log(src_all)
        log_tgt[...] = jnp.log(tgt_mass[...].astype(jnp.float32)) - jnp.log(tgt_all)

    def merge_src(it):
        tp = send_src.shape[1]
        first = []
        for off in range(n_col):
            peer = lax.rem(col + 1 + off, n_col)
            for u in range(tp):
                send_src[peer, u : u + 1, :] = runs[pl.ds(idx[2, peer * tp + u], 1), :]
            if off < n_col - 1:
                first.append(send(
                    "col", col, n_col, off + 1,
                    send_src.at[peer], got_src.at[it, col], src_sems.at[it, 0],
                ))
        pl.when(it == 0)(mass_logs)
        for copy in first:
            copy.wait_recv()
        parts = [send_src[col]] + [
            got_src[it, lax.rem(col + off, n_col)] for off in range(1, n_col)
        ]
        hat_src[it, col] = (log_src[...] - merged(parts)) * (1.0 / COST)
        mine = hat_src.at[it, col]
        second = [
            send("col", col, n_col, off, mine, mine, src_sems.at[it, 1])
            for off in range(1, n_col)
        ]
        for copy in second:
            copy.wait_recv()
        for copy in first + second:
            copy.wait_send()

    def merge_tgt(it):
        tiles = got_tgt.shape[2]

        def pick(block, carry):
            for u in range(UNROLL):
                t = block * UNROLL + u
                got_tgt[it, row, pl.ds(t, 1), :] = runs[pl.ds(idx[5, t], 1), :]
            return carry

        lax.fori_loop(0, tiles // UNROLL, pick, 0)
        mine = got_tgt.at[it, row]
        copies = [
            send("row", row, n_row, off, mine, mine, tgt_sems.at[it]) for off in range(1, n_row)
        ]
        @pl.when(it == ITERS - 1)
        def _():
            src_hat = hat_src[ITERS - 1].reshape(sq_src.shape)
            src_out[...] = (src_hat + sq_src[...]) * COST

        for copy in copies:
            copy.wait()
        parts = [got_tgt[it, r] for r in range(n_row)]
        hat_tgt[it + 1] = (log_tgt[...] - merged(parts)) * (1.0 / COST)

    def iterate(it, carry):
        partials(lambda t: hat_tgt[it, pl.ds(t, 1), :], a_tgt, b_src, 1, 0, place_s)
        merge_src(it)
        tp = hat_src.shape[2]
        partials(
            lambda t: hat_src[it, t // tp, pl.ds(t % tp, 1), :], a_src, b_tgt, 4, 3, place_t
        )
        merge_tgt(it)
        return carry

    lax.fori_loop(0, ITERS, iterate, 0)
    tgt_out[...] = (hat_tgt[ITERS] + sq_tgt[...]) * COST


def on_device(
    n_row, n_col,
    src_coords, tgt_coords, src_mass, tgt_mass, tgt_start, kept_src, kept_tgt, kept_count,
):
    slots = kept_src.shape[-1]
    src_tiles, tgt_tiles = src_coords.shape[1] // LANES, tgt_coords.shape[1] // LANES
    src_split = (n_col, src_tiles // n_col, LANES)
    src_block, tgt_block = (src_tiles, LANES), (tgt_tiles, LANES)
    f32, i32 = jnp.float32, jnp.int32
    src_out, tgt_out = pl.pallas_call(
        functools.partial(kernel, n_row, n_col),
        out_shape=(
            jax.ShapeDtypeStruct(src_block, f32),
            jax.ShapeDtypeStruct(tgt_block, f32),
        ),
        in_specs=[pl.BlockSpec(memory_space=pl.ANY)] * 8,
        out_specs=(pl.BlockSpec(memory_space=pltpu.VMEM),) * 2,
        scratch_shapes=[
            pltpu.VMEM((1, 1), i32),
            pltpu.VMEM((1, slots), i32),
            pltpu.VMEM((1, slots), i32),
            pltpu.VMEM(src_coords.shape, i32),
            pltpu.VMEM(tgt_coords.shape, i32),
            pltpu.VMEM(src_split, i32),
            pltpu.VMEM(tgt_block, i32),
            pltpu.VMEM(tgt_block, f32),
            pltpu.SemaphoreType.DMA((8,)),
            pltpu.VMEM((8, LANES), i32),
            pltpu.SMEM((8, LANES), i32),
            pltpu.SemaphoreType.DMA,
            pltpu.VMEM((slots, LANES), i32),
            pltpu.VMEM((slots, LANES), i32),
            pltpu.VMEM((src_tiles, 8, LANES), f32),
            pltpu.VMEM((src_tiles, 8, LANES), f32),
            pltpu.VMEM((tgt_tiles, 8, LANES), f32),
            pltpu.VMEM((tgt_tiles, 8, LANES), f32),
            pltpu.VMEM(src_block, f32),
            pltpu.VMEM(tgt_block, f32),
            pltpu.VMEM(src_split[1:], f32),
            pltpu.VMEM(tgt_block, f32),
            pltpu.VMEM((ITERS,) + src_split, f32),
            pltpu.VMEM((ITERS + 1,) + tgt_block, f32),
            pltpu.VMEM((slots, LANES), f32),
            pltpu.VMEM((slots, LANES), f32),
            pltpu.VMEM((slots + 8, LANES), f32),
            pltpu.VMEM(src_split, f32),
            pltpu.VMEM((ITERS,) + src_split, f32),
            pltpu.VMEM((ITERS, n_row) + tgt_block, f32),
            pltpu.VMEM((n_row, 8, LANES), f32),
            pltpu.VMEM((n_col, 8, LANES), f32),
            pltpu.SemaphoreType.DMA((2, n_row + n_col - 2)),
            pltpu.SemaphoreType.DMA((ITERS, 2, 2, n_col - 1)),
            pltpu.SemaphoreType.DMA((ITERS, 2, n_row - 1)),
        ],
        compiler_params=pltpu.CompilerParams(
            collective_id=0, has_side_effects=True, vmem_limit_bytes=56 * 1024 * 1024
        ),
        name="sinkhorn",
    )(
        kept_count, kept_src.reshape(1, slots), kept_tgt.reshape(1, slots),
        src_coords, tgt_coords,
        src_mass.reshape(src_split), tgt_mass.reshape(tgt_block), tgt_start.reshape(tgt_block),
    )
    return src_out.reshape(-1), tgt_out.reshape(-1)


def solution(mesh):
    placed = (
        P(None, "row"), P(None, "col"), P("row"), P("col"), P("col"),
        P("row", "col", None), P("row", "col", None), P("row", "col"),
    )
    return jax.shard_map(
        functools.partial(on_device, mesh.shape["row"], mesh.shape["col"]),
        mesh=mesh, in_specs=placed, out_specs=(P("row"), P("col")), check_vma=False,
    )
```
